512 devices in a mesh: seq: 32 (over z, x), tensor: 16 (over y, core).
Axes of the slice: x: 4, y: 8, z: 8, core: 2. Of those that a mesh axis runs over, the one named last changes fastest.
Arguments:
- queries: bfloat16 [65536, 4096], P('seq', 'tensor'), may hold values from -30 to 30
- latents: bfloat16 [32, 64, 1280], P('seq'), may hold values from -6 to 6
- key_weight: bfloat16 [1280, 4096], P('seq', 'tensor'), may hold values from -0.15625 to 0.15625
- value_weight: bfloat16 [1280, 4096], P('seq', 'tensor'), may hold values from -0.15625 to 0.15625
- grad_out: bfloat16 [65536, 4096], P('seq', 'tensor'), may hold values from -6 to 6
- pairs: int32 [256, 4], P('seq'), may hold values from -1 to 31, as said below
- image_slot: int32 [32], replicated, may hold values from 0 to 31, each once
- token_doc: int32 [65536], P('seq'), may hold values from 0 to 7, as said below
Outputs:
- attended: bfloat16 [65536, 4096], P('seq', 'tensor')
- grad_queries: bfloat16 [65536, 4096], P('seq', 'tensor')
- grad_latents: bfloat16 [32, 64, 1280], P('seq')
The draws below stay inside these ranges and needn't reach their ends.
Inputs may be any that keep to these rules, and one draw needn't show every extreme that they name: `pairs`: row c lists the images whose latents group c attends; -1 marks an empty slot, empty slots come last, listed images of a row are distinct, image i belongs to document i // 4; every token's document has an image listed in its group's row; some row is full. How many images a row lists is very uneven from device to device. `token_doc`: documents are runs of tokens in order, of uneven lengths; a group holds tokens of at most two documents.
All inputs are finite; a program needn't handle non-finite values.
Results may differ from the reference program's by a relative error of at most 0.029.
Values may be sent and summed in bfloat16 or wider, within the bound.
No kernel may reach another device: no remote copies, remote signals or barrier semaphores. Data moves between devices by JAX's collectives and lax.ppermute only.
A program may use at most 64 MiB of HBM per device.

```python
import jax
import jax.numpy as jnp
from jax import lax

VIS = 1280
HEADS = 32
HEAD = 128
LAT = 64
TOK_DEV = 2048
GROUP = 256
MAXP = 4
IMAGES = 32
DOCS = 8
IPD = 4
HD = 4096
TOKENS = 65536
GROUPS = 256
N_SEQ = 32


def group_plan(key):
    keys_list = jax.random.split(key, 8)
    doc_index = jnp.arange(DOCS, dtype=jnp.int32)
    weights = jax.random.randint(keys_list[0], (DOCS,), 1, 9)
    long_doc = jax.random.randint(keys_list[7], (), 0, DOCS)
    weights = jnp.where(doc_index == long_doc, 48, weights).astype(jnp.int32)
    spare = TOKENS - DOCS * GROUP
    extra = spare * weights // jnp.sum(weights)
    lengths = GROUP + extra
    lengths = jnp.where(doc_index == DOCS - 1, TOKENS - (jnp.sum(lengths) - lengths[DOCS - 1]), lengths)
    starts = (jnp.cumsum(lengths) - lengths).astype(jnp.int32)
    positions = jnp.arange(TOKENS, dtype=jnp.int32)
    token_doc = jnp.sum((positions[:, None] >= starts[None, :]).astype(jnp.int32), axis=1) - 1
    by_group = token_doc.reshape(GROUPS, GROUP)
    first_doc = by_group[:, 0]
    last_doc = by_group[:, GROUP - 1]
    first_pick = jax.random.randint(keys_list[1], (GROUPS,), 0, IPD)
    shift_pick = jax.random.randint(keys_list[2], (GROUPS,), 0, IPD - MAXP + 1)
    slot_index = jnp.arange(MAXP, dtype=jnp.int32)
    later = last_doc[:, None] * IPD + (first_pick[:, None] + shift_pick[:, None] + slot_index[None, :]) % IPD
    image_ids = jnp.where(slot_index[None, :] == 0, (first_doc * IPD + first_pick)[:, None], later)
    heavy_device = jax.random.randint(keys_list[3], (N_SEQ,), 0, 4) == 0
    group_index = jnp.arange(GROUPS, dtype=jnp.int32)
    heavy_group = heavy_device[group_index // (TOK_DEV // GROUP)]
    heavy_count = jax.random.randint(keys_list[4], (GROUPS,), MAXP // 2, MAXP + 1)
    light_count = jax.random.randint(keys_list[5], (GROUPS,), 1, 3)
    counts = jnp.where(heavy_group, heavy_count, light_count)
    counts = jnp.where(first_doc != last_doc, jnp.maximum(counts, 2), counts)
    full_row = jax.random.randint(keys_list[6], (), 0, GROUPS)
    counts = jnp.where(group_index == full_row, MAXP, counts)
    pairs = jnp.where(slot_index[None, :] < counts[:, None], image_ids, -1)
    return (token_doc.astype(jnp.int32), pairs.astype(jnp.int32))


def draw_pairs(key, part):
    plan = group_plan(key)
    return plan[1]


def draw_token_doc(key, part):
    plan = group_plan(key)
    return plan[0]


def draw_queries(key, part):
    key = jax.random.fold_in(key, 3)
    first_key = jax.random.fold_in(key, 0)
    values = jnp.clip(jax.random.normal(first_key, (TOKENS, HD), jnp.float32), -6.0, 6.0)
    return values.astype(jnp.bfloat16)


def level_of(stream_key, extent, cuts, smallest, high):
    def one(position, shards_of):
        steps = jax.random.uniform(jax.random.fold_in(jax.random.fold_in(stream_key, 6), position), (shards_of,), jnp.float32, smallest / len(cuts), high / len(cuts))
        return jnp.repeat(jnp.exp(steps), extent[position] // shards_of).reshape((-1,) + (1,) * (len(extent) - position - 1))

    factor_of = one(*cuts[0])
    for cut in cuts[1:]:
        factor_of = factor_of * one(*cut)
    return factor_of


def noise(key, dims, deviation, most, pieces=(), held_as=jnp.bfloat16):
    drawn = jax.random.normal(key, dims, jnp.float32) * deviation
    if len(pieces) > 0:
        drawn = level_of(key, dims, pieces, -0.22, 0.18) * drawn
    return jnp.clip(drawn, min=-most, max=most).astype(held_as)


def setup_inputs(seed: int = 0) -> dict:
    splits = jax.random.split(jax.random.key(seed), 9)
    queries = draw_queries(jax.random.fold_in(splits[8], 71), 0)
    latents = noise(splits[1], (IMAGES, LAT, VIS), 1.0, 6.0, ((0, 32),))
    key_weight = noise(splits[2], (VIS, HD), VIS ** -0.5, 0.15625, ((0, 32), (1, 16)))
    value_weight = noise(splits[3], (VIS, HD), VIS ** -0.5, 0.15625, ((0, 32), (1, 16)))
    grad_out = noise(splits[4], (TOKENS, HD), 1.0, 6.0, ((0, 32), (1, 16)))
    pairs = draw_pairs(jax.random.fold_in(splits[8], 71), 0)
    image_slot = jax.random.permutation(splits[6], IMAGES).astype(jnp.int32)
    token_doc = draw_token_doc(jax.random.fold_in(splits[8], 71), 0)
    return {"queries": queries, "latents": latents, "key_weight": key_weight, "value_weight": value_weight, "grad_out": grad_out, "pairs": pairs, "image_slot": image_slot, "token_doc": token_doc}


MASKED_SCORE = -1.0e30


def lookup(slot_table, image_ids):
    matches = image_ids[..., None] == jnp.arange(slot_table.shape[0], dtype=jnp.int32)
    return jnp.sum(jnp.where(matches, slot_table, 0), axis=-1).astype(jnp.int32)


def softmax_probs(query_block, key_rows, visible, score_scale):
    scores = jnp.einsum("cthd,ckhd->chtk", query_block.astype(jnp.float32), key_rows.astype(jnp.float32)) * score_scale
    scores = jnp.where(visible, scores, MASKED_SCORE)
    row_max = jnp.max(scores, axis=-1, keepdims=True)
    exponent = jnp.where(visible, jnp.exp(scores - row_max), 0.0)
    return exponent / jnp.sum(exponent, axis=-1, keepdims=True)


def reference(queries, latents, key_weight, value_weight, grad_out, pairs, image_slot, token_doc):
    flat_latents = latents.reshape(IMAGES * LAT, VIS)
    key_proj = jnp.dot(flat_latents, key_weight, preferred_element_type=jnp.float32).astype(jnp.bfloat16)
    value_proj = jnp.dot(flat_latents, value_weight, preferred_element_type=jnp.float32).astype(jnp.bfloat16)
    group_count = TOK_DEV // GROUP
    score_scale = HEAD ** -0.5
    pair_blocks = pairs.reshape(N_SEQ, group_count, MAXP)
    query_blocks = queries.reshape(N_SEQ, group_count, GROUP, HEADS, HEAD)
    grad_blocks = grad_out.reshape(N_SEQ, group_count, GROUP, HEADS, HEAD)
    doc_blocks = token_doc.reshape(N_SEQ, group_count, GROUP)

    def one_block(running, inputs):
        image_ids, query_block, cotangent, token_docs = inputs
        slot_ids = lookup(image_slot, image_ids)
        key_index = (slot_ids[:, :, None] * LAT + jnp.arange(LAT, dtype=jnp.int32)).reshape(group_count, MAXP * LAT)
        key_rows = key_proj[key_index].reshape(group_count, MAXP * LAT, HEADS, HEAD)
        value_rows = value_proj[key_index].reshape(group_count, MAXP * LAT, HEADS, HEAD)
        visible = (image_ids >= 0)[:, None, :] & ((image_ids // IPD)[:, None, :] == token_docs[:, :, None])
        visible = jnp.repeat(visible, LAT, axis=2)[:, None]
        attn_prob = softmax_probs(query_block, key_rows, visible, score_scale)
        prob_low = attn_prob.astype(jnp.bfloat16)
        attended = jnp.einsum("chtk,ckhd->cthd", prob_low.astype(jnp.float32), value_rows.astype(jnp.float32)).astype(jnp.bfloat16)
        prob_grad = jnp.einsum("cthd,ckhd->chtk", cotangent.astype(jnp.float32), value_rows.astype(jnp.float32))
        centre = jnp.sum(attn_prob * prob_grad, axis=-1, keepdims=True)
        score_grad = (attn_prob * (prob_grad - centre) * score_scale).astype(jnp.bfloat16)
        grad_query = jnp.einsum("chtk,ckhd->cthd", score_grad.astype(jnp.float32), key_rows.astype(jnp.float32)).astype(jnp.bfloat16)
        key_grad_rows = jnp.einsum("chtk,cthd->ckhd", score_grad.astype(jnp.float32), query_block.astype(jnp.float32))
        value_grad_rows = jnp.einsum("chtk,cthd->ckhd", prob_low.astype(jnp.float32), cotangent.astype(jnp.float32))
        onehot = ((slot_ids[:, :, None] == jnp.arange(IMAGES, dtype=jnp.int32)) & (image_ids >= 0)[:, :, None])
        onehot = onehot.astype(jnp.float32).reshape(group_count * MAXP, IMAGES)
        key_term = jnp.einsum("ps,plx->slx", onehot, key_grad_rows.reshape(group_count * MAXP, LAT, HD), precision=lax.Precision.HIGHEST)
        value_term = jnp.einsum("ps,plx->slx", onehot, value_grad_rows.reshape(group_count * MAXP, LAT, HD), precision=lax.Precision.HIGHEST)
        key_low = lax.optimization_barrier(key_term.reshape(IMAGES * LAT, HD).astype(jnp.bfloat16))
        value_low = lax.optimization_barrier(value_term.reshape(IMAGES * LAT, HD).astype(jnp.bfloat16))
        running = (running[0] + key_low.astype(jnp.float32), running[1] + value_low.astype(jnp.float32))
        return running, (attended.reshape(group_count, GROUP, HD), grad_query.reshape(group_count, GROUP, HD))

    start_sums = (jnp.zeros((IMAGES * LAT, HD), jnp.float32), jnp.zeros((IMAGES * LAT, HD), jnp.float32))
    totals, outputs = lax.scan(one_block, start_sums, (pair_blocks, query_blocks, grad_blocks, doc_blocks))
    attended = outputs[0].reshape(TOKENS, HD)
    grad_queries = outputs[1].reshape(TOKENS, HD)
    key_grad = totals[0].astype(jnp.bfloat16)
    value_grad = totals[1].astype(jnp.bfloat16)
    latent_sum = jnp.dot(key_grad, key_weight.T, preferred_element_type=jnp.float32)
    latent_sum = latent_sum + jnp.dot(value_grad, value_weight.T, preferred_element_type=jnp.float32)
    grad_latents = latent_sum.reshape(IMAGES, LAT, VIS).astype(jnp.bfloat16)
    return attended, grad_queries, grad_latents
```

```python
import jax
import jax.numpy as jnp
from jax import lax
from jax.experimental import pallas as pl
from jax.experimental.pallas import tpu as pltpu
from jax.sharding import Mesh
from jax.sharding import PartitionSpec as P

HEAD = 128
LAT = 64
GROUP = 256
GROUPS = 8
SLOTS = 4
IPD = 4
NX = 4
NZ = 8
NT = 16
COLS = 256
WIDE = 2 * COLS
VIS = 1280
IMAGES = 32
MASKED = -1.0e30
SCALE = HEAD ** -0.5
LOG2E = 1.4426950408889634

NT_DIMS = (((1,), (1,)), ((), ()))
TN_DIMS = (((0,), (0,)), ((), ()))


def attention_kernel(rel_ref, abs_ref, doc_ref, tok_ref, q_ref, g_ref, p0, p1, p2, p3,
                     att_ref, dq_ref, dkv_ref, kv, acc, sem):
    group = pl.program_id(0)

    @pl.when(group == 0)
    def _():
        copies = [
            pltpu.make_async_copy(piece, kv.at[pl.ds(i * NZ, NZ)], sem.at[i])
            for i, piece in enumerate((p0, p1, p2, p3))
        ]
        for copy in copies:
            copy.start()
        acc[...] = jnp.zeros_like(acc)
        for copy in copies:
            copy.wait()

    tok = tok_ref[0]
    rel = [rel_ref[group, j] for j in range(SLOTS)]
    dst = [abs_ref[group, j] for j in range(SLOTS)]
    bias = [jnp.where(tok == doc_ref[group, j], 0.0, MASKED) for j in range(SLOTS)]
    bias = jnp.concatenate([jnp.broadcast_to(b, (LAT, GROUP)) for b in bias], axis=0)
    for head in range(COLS // HEAD):
        lo = head * HEAD
        k = jnp.concatenate([kv[r, :, lo:lo + HEAD] for r in rel], axis=0)
        v = jnp.concatenate([kv[r, :, COLS + lo:COLS + lo + HEAD] for r in rel], axis=0)
        q = q_ref[:, lo:lo + HEAD]
        g = g_ref[:, lo:lo + HEAD]
        s = lax.dot_general(k, q, NT_DIMS, preferred_element_type=jnp.float32) + bias
        top = jnp.max(s, axis=0, keepdims=True)
        e = jnp.exp2((s - top) * (SCALE * LOG2E))
        p = e * (1.0 / jnp.sum(e, axis=0, keepdims=True))
        low = p.astype(jnp.bfloat16)
        dp = lax.dot_general(v, g, NT_DIMS, preferred_element_type=jnp.float32)
        centre = jnp.sum(p * dp, axis=0, keepdims=True)
        sg = (p * (dp - centre) * SCALE).astype(jnp.bfloat16)
        att = lax.dot_general(low, v, TN_DIMS, preferred_element_type=jnp.float32)
        dq = lax.dot_general(sg, k, TN_DIMS, preferred_element_type=jnp.float32)
        att_ref[:, lo:lo + HEAD] = att.astype(jnp.bfloat16)
        dq_ref[:, lo:lo + HEAD] = dq.astype(jnp.bfloat16)
        dk = jnp.dot(sg, q, preferred_element_type=jnp.float32)
        dv = jnp.dot(low, g, preferred_element_type=jnp.float32)
        for j in range(SLOTS):
            rows = slice(j * LAT, (j + 1) * LAT)
            acc[dst[j], :, lo:lo + HEAD] += dk[rows]
            acc[dst[j], :, COLS + lo:COLS + lo + HEAD] += dv[rows]

    @pl.when(group == GROUPS - 1)
    def _():
        dkv_ref[...] = acc[...].astype(jnp.bfloat16)


def attention(rel, dst, docs, tok, queries, grad_out, pieces):
    tokens = queries.shape[0]
    block = pl.BlockSpec((GROUP, COLS), lambda g, *_: (g, 0))
    return pl.pallas_call(
        attention_kernel,
        grid_spec=pltpu.PrefetchScalarGridSpec(
            num_scalar_prefetch=3,
            grid=(GROUPS,),
            in_specs=[
                pl.BlockSpec((1, 1, GROUP), lambda g, *_: (g, 0, 0)),
                block,
                block,
            ] + [pl.BlockSpec(memory_space=pl.ANY)] * NX,
            out_specs=[
                block,
                block,
                pl.BlockSpec((IMAGES, LAT, WIDE), lambda g, *_: (0, 0, 0)),
            ],
            scratch_shapes=[
                pltpu.VMEM((IMAGES, LAT, WIDE), jnp.bfloat16),
                pltpu.VMEM((IMAGES, LAT, WIDE), jnp.float32),
                pltpu.SemaphoreType.DMA((NX,)),
            ],
        ),
        out_shape=[
            jax.ShapeDtypeStruct((tokens, COLS), jnp.bfloat16),
            jax.ShapeDtypeStruct((tokens, COLS), jnp.bfloat16),
            jax.ShapeDtypeStruct((IMAGES, LAT, WIDE), jnp.bfloat16),
        ],
        compiler_params=pltpu.CompilerParams(
            dimension_semantics=("arbitrary",), vmem_limit_bytes=40 * 2**20
        ),
        cost_estimate=pl.CostEstimate(
            flops=12 * tokens * GROUP * COLS, bytes_accessed=9 * 2**20, transcendentals=0
        ),
    )(rel, dst, docs, tok, queries, grad_out, *pieces)


def from_offset(value, axis, size, step):
    return lax.ppermute(value, axis, [(i, (i - step) % size) for i in range(size)])


def local(queries, latents, key_weight, value_weight, grad_out, pairs, image_slot, token_doc):
    x = lax.axis_index("x")
    z = lax.axis_index("z")
    weight = jnp.concatenate([key_weight, value_weight], axis=1)
    weight = lax.all_gather(weight, "x", axis=0, tiled=True)
    weight = lax.all_gather(weight, "z", axis=0, tiled=True)
    kv = jnp.dot(latents[0], weight, preferred_element_type=jnp.float32).astype(jnp.bfloat16)
    column = jnp.stack([kv] + [from_offset(kv, "z", NZ, i) for i in range(1, NZ)])
    pieces = [column] + [from_offset(column, "x", NX, i) for i in range(1, NX)]

    matches = pairs[..., None] == jnp.arange(IMAGES, dtype=jnp.int32)
    slot = jnp.sum(jnp.where(matches, image_slot, 0), axis=-1).astype(jnp.int32)
    slot_z, slot_x = slot // NX, slot % NX
    rel = (slot_x - x) % NX * NZ + (slot_z - z) % NZ
    dst = slot_x * NZ + slot_z
    docs = jnp.where(pairs >= 0, pairs // IPD, -1)
    tok = token_doc.reshape(GROUPS, 1, GROUP)
    attended, grad_queries, dkv = attention(rel, dst, docs, tok, queries, grad_out, pieces)

    dkv = dkv.reshape(NX, NZ, LAT, WIDE)
    dkv = lax.all_to_all(dkv, "x", 0, 0, tiled=True)
    dkv = jnp.sum(dkv.astype(jnp.float32), axis=0).astype(jnp.bfloat16)
    dkv = lax.all_to_all(dkv, "z", 0, 0, tiled=True)
    dkv = jnp.sum(dkv.astype(jnp.float32), axis=0).astype(jnp.bfloat16)

    term = lax.dot_general(dkv, weight, NT_DIMS, preferred_element_type=jnp.float32)
    term = term.astype(jnp.bfloat16).reshape(NT, LAT // NT, VIS)
    term = lax.all_to_all(term, ("y", "core"), 0, 0, tiled=True)
    term = jnp.sum(term.astype(jnp.float32), axis=0).astype(jnp.bfloat16)
    term = lax.all_gather(term, ("y", "core"), axis=0, tiled=True)
    return attended, grad_queries, term[None]


def solution(mesh):
    fine = Mesh(mesh.devices.reshape(NZ, NX, NT // 2, 2), ("z", "x", "y", "core"))
    seq, tensor = ("z", "x"), ("y", "core")
    in_specs = (
        P(seq, tensor),
        P(seq, None, None),
        P(seq, tensor),
        P(seq, tensor),
        P(seq, tensor),
        P(seq, None),
        P(),
        P(seq),
    )
    out_specs = (P(seq, tensor), P(seq, tensor), P(seq, None, None))
    return jax.shard_map(local, mesh=fine, in_specs=in_specs, out_specs=out_specs, check_vma=False)
```

```python
import jax
import jax.numpy as jnp
from jax import lax
from jax.experimental import pallas as pl
from jax.experimental.pallas import tpu as pltpu
from jax.sharding import Mesh
from jax.sharding import PartitionSpec as P

HEAD = 128
LAT = 64
GROUP = 256
GROUPS = 8
SLOTS = 4
IPD = 4
NX = 4
NZ = 8
NY = 8
WROWS = 40
COLS = 256
WIDE = 2 * COLS
VIS = 1280
IMAGES = 32
MASKED = -1.0e30
SCALE = HEAD ** -0.5
LOG2E = 1.4426950408889634

NT_DIMS = (((1,), (1,)), ((), ()))
TN_DIMS = (((0,), (0,)), ((), ()))


def attention_kernel(rel_ref, abs_ref, doc_ref, tok_ref, q_ref, g_ref, p0, p1, p2, p3,
                     att_ref, dq_ref, dkv_ref, kv, acc, sem):
    group = pl.program_id(0)

    @pl.when(group == 0)
    def _():
        copies = [
            pltpu.make_async_copy(piece, kv.at[pl.ds(i * NZ, NZ)], sem.at[i])
            for i, piece in enumerate((p0, p1, p2, p3))
        ]
        for copy in copies:
            copy.start()
        acc[...] = jnp.zeros_like(acc)
        for copy in copies:
            copy.wait()

    tok = tok_ref[0]
    rel = [rel_ref[group, j] for j in range(SLOTS)]
    dst = [abs_ref[group, j] for j in range(SLOTS)]
    bias = [jnp.where(tok == doc_ref[group, j], 0.0, MASKED) for j in range(SLOTS)]
    bias = jnp.concatenate([jnp.broadcast_to(b, (LAT, GROUP)) for b in bias], axis=0)
    for head in range(COLS // HEAD):
        lo = head * HEAD
        k = jnp.concatenate([kv[r, :, lo:lo + HEAD] for r in rel], axis=0)
        v = jnp.concatenate([kv[r, :, COLS + lo:COLS + lo + HEAD] for r in rel], axis=0)
        q = q_ref[:, lo:lo + HEAD]
        g = g_ref[:, lo:lo + HEAD]
        s = lax.dot_general(k, q, NT_DIMS, preferred_element_type=jnp.float32) + bias
        top = jnp.max(s, axis=0, keepdims=True)
        e = jnp.exp2((s - top) * (SCALE * LOG2E))
        p = e * (1.0 / jnp.sum(e, axis=0, keepdims=True))
        low = p.astype(jnp.bfloat16)
        dp = lax.dot_general(v, g, NT_DIMS, preferred_element_type=jnp.float32)
        centre = jnp.sum(p * dp, axis=0, keepdims=True)
        sg = (p * (dp - centre) * SCALE).astype(jnp.bfloat16)
        att = lax.dot_general(low, v, TN_DIMS, preferred_element_type=jnp.float32)
        dq = lax.dot_general(sg, k, TN_DIMS, preferred_element_type=jnp.float32)
        att_ref[:, lo:lo + HEAD] = att.astype(jnp.bfloat16)
        dq_ref[:, lo:lo + HEAD] = dq.astype(jnp.bfloat16)
        dk = jnp.dot(sg, q, preferred_element_type=jnp.float32)
        dv = jnp.dot(low, g, preferred_element_type=jnp.float32)
        for j in range(SLOTS):
            rows = slice(j * LAT, (j + 1) * LAT)
            acc[dst[j], :, lo:lo + HEAD] += dk[rows]
            acc[dst[j], :, COLS + lo:COLS + lo + HEAD] += dv[rows]

    @pl.when(group == GROUPS - 1)
    def _():
        dkv_ref[...] = acc[...].astype(jnp.bfloat16)


def attention(rel, dst, docs, tok, queries, grad_out, pieces):
    tokens = queries.shape[0]
    block = pl.BlockSpec((GROUP, COLS), lambda g, *_: (g, 0))
    return pl.pallas_call(
        attention_kernel,
        grid_spec=pltpu.PrefetchScalarGridSpec(
            num_scalar_prefetch=3,
            grid=(GROUPS,),
            in_specs=[
                pl.BlockSpec((1, 1, GROUP), lambda g, *_: (g, 0, 0)),
                block,
                block,
            ] + [pl.BlockSpec(memory_space=pl.ANY)] * NX,
            out_specs=[
                block,
                block,
                pl.BlockSpec((IMAGES, LAT, WIDE), lambda g, *_: (0, 0, 0)),
            ],
            scratch_shapes=[
                pltpu.VMEM((IMAGES, LAT, WIDE), jnp.bfloat16),
                pltpu.VMEM((IMAGES, LAT, WIDE), jnp.float32),
                pltpu.SemaphoreType.DMA((NX,)),
            ],
        ),
        out_shape=[
            jax.ShapeDtypeStruct((tokens, COLS), jnp.bfloat16),
            jax.ShapeDtypeStruct((tokens, COLS), jnp.bfloat16),
            jax.ShapeDtypeStruct((IMAGES, LAT, WIDE), jnp.bfloat16),
        ],
        compiler_params=pltpu.CompilerParams(
            dimension_semantics=("arbitrary",), vmem_limit_bytes=40 * 2**20
        ),
        cost_estimate=pl.CostEstimate(
            flops=12 * tokens * GROUP * COLS, bytes_accessed=9 * 2**20, transcendentals=0
        ),
    )(rel, dst, docs, tok, queries, grad_out, *pieces)


def from_offset(value, axis, size, step):
    return lax.ppermute(value, axis, [(i, (i - step) % size) for i in range(size)])


def local(queries, latents, key_weight, value_weight, grad_out, pairs, image_slot, token_doc):
    x = lax.axis_index("x")
    core = lax.axis_index("core")

    weight = jnp.concatenate([key_weight, value_weight], axis=1)
    part = lax.all_gather(weight, "z", axis=0, tiled=True)
    own = latents[0].reshape(LAT, NZ, NX, WROWS).transpose(2, 0, 1, 3).reshape(NX, LAT, NZ * WROWS)
    row = lax.all_to_all(own, "x", 0, 0, tiled=True)
    kv = jnp.einsum("jlv,vc->jlc", row, part, preferred_element_type=jnp.float32)
    kv = lax.all_to_all(kv.astype(jnp.bfloat16), "x", 0, 0, tiled=True)
    kv = jnp.sum(kv.astype(jnp.float32), axis=0).astype(jnp.bfloat16)
    column = lax.all_gather(kv, "z", axis=0)
    pieces = [column] + [from_offset(column, "x", NX, i) for i in range(1, NX)]

    whole = lax.all_gather(part, "x", axis=0)
    whole = whole.reshape(NX, NZ, WROWS, WIDE).transpose(1, 0, 2, 3).reshape(VIS, WIDE)

    matches = pairs[..., None] == jnp.arange(IMAGES, dtype=jnp.int32)
    slot = jnp.sum(jnp.where(matches, image_slot, 0), axis=-1).astype(jnp.int32)
    slot_z, slot_x = slot // NX, slot % NX
    rel = (slot_x - x) % NX * NZ + slot_z
    dst = slot_x * NZ + slot_z
    docs = jnp.where(pairs >= 0, pairs // IPD, -1)
    tok = token_doc.reshape(GROUPS, 1, GROUP)
    attended, grad_queries, dkv = attention(rel, dst, docs, tok, queries, grad_out, pieces)

    dkv = dkv.reshape(NX, NZ, LAT, WIDE)
    dkv = lax.all_to_all(dkv, "x", 0, 0, tiled=True)
    dkv = jnp.sum(dkv.astype(jnp.float32), axis=0).astype(jnp.bfloat16)
    dkv = lax.all_to_all(dkv, "z", 0, 0, tiled=True)
    dkv = jnp.sum(dkv.astype(jnp.float32), axis=0).astype(jnp.bfloat16)

    term = lax.dot_general(dkv, whole, NT_DIMS, preferred_element_type=jnp.float32)
    half = LAT // 2
    keep = jnp.where(core == 0, term[:half], term[half:])
    give = jnp.where(core == 0, term[half:], term[:half]).astype(jnp.bfloat16)
    term = keep + from_offset(give, "core", 2, 1).astype(jnp.float32)
    term = term.astype(jnp.bfloat16).reshape(NY, half // NY, VIS)
    term = lax.all_to_all(term, "y", 0, 0, tiled=True)
    term = jnp.sum(term.astype(jnp.float32), axis=0).astype(jnp.bfloat16)
    term = lax.all_gather(term, "y", axis=0, tiled=True)
    other = from_offset(term, "core", 2, 1)
    first = jnp.where(core == 0, term, other)
    second = jnp.where(core == 0, other, term)
    return attended, grad_queries, jnp.concatenate([first, second])[None]


def solution(mesh):
    fine = Mesh(mesh.devices.reshape(NZ, NX, NY, 2), ("z", "x", "y", "core"))
    seq, tensor = ("z", "x"), ("y", "core")
    in_specs = (
        P(seq, tensor),
        P(seq, None, None),
        P(seq, tensor),
        P(seq, tensor),
        P(seq, tensor),
        P(seq, None),
        P(),
        P(seq),
    )
    out_specs = (P(seq, tensor), P(seq, tensor), P(seq, None, None))
    return jax.shard_map(local, mesh=fine, in_specs=in_specs, out_specs=out_specs, check_vma=False)
```

```python
import jax
import jax.numpy as jnp
from jax import lax
from jax.experimental import pallas as pl
from jax.experimental.pallas import tpu as pltpu
from jax.sharding import Mesh
from jax.sharding import PartitionSpec as P

HEAD = 128
LAT = 64
GROUP = 256
GROUPS = 8
SLOTS = 4
IPD = 4
NX = 4
NZ = 8
NY = 8
WROWS = 40
COLS = 256
WIDE = 2 * COLS
VIS = 1280
IMAGES = 32
MASKED = -1.0e30
SCALE = HEAD ** -0.5
LOG2E = 1.4426950408889634

NT_DIMS = (((1,), (1,)), ((), ()))
TN_DIMS = (((0,), (0,)), ((), ()))


def attention_kernel(rel_ref, abs_ref, doc_ref, tok_ref, q_ref, g_ref, p0, p1, p2, p3,
                     att_ref, dq_ref, dkv_ref, kv, acc, sem):
    group = pl.program_id(0)

    @pl.when(group == 0)
    def _():
        copies = [
            pltpu.make_async_copy(piece, kv.at[pl.ds(i * NZ, NZ)], sem.at[i])
            for i, piece in enumerate((p0, p1, p2, p3))
        ]
        for copy in copies:
            copy.start()
        acc[...] = jnp.zeros_like(acc)
        for copy in copies:
            copy.wait()

    tok = tok_ref[0]
    rel = [rel_ref[group, j] for j in range(SLOTS)]
    dst = [abs_ref[group, j] for j in range(SLOTS)]
    bias = [jnp.where(tok == doc_ref[group, j], 0.0, MASKED) for j in range(SLOTS)]
    bias = jnp.concatenate([jnp.broadcast_to(b, (LAT, GROUP)) for b in bias], axis=0)
    for head in range(COLS // HEAD):
        lo = head * HEAD
        k = jnp.concatenate([kv[r, :, lo:lo + HEAD] for r in rel], axis=0)
        v = jnp.concatenate([kv[r, :, COLS + lo:COLS + lo + HEAD] for r in rel], axis=0)
        q = q_ref[:, lo:lo + HEAD]
        g = g_ref[:, lo:lo + HEAD]
        s = lax.dot_general(k, q, NT_DIMS, preferred_element_type=jnp.float32) + bias
        top = jnp.max(s, axis=0, keepdims=True)
        e = jnp.exp2((s - top) * (SCALE * LOG2E))
        p = e * (1.0 / jnp.sum(e, axis=0, keepdims=True))
        low = p.astype(jnp.bfloat16)
        dp = lax.dot_general(v, g, NT_DIMS, preferred_element_type=jnp.float32)
        centre = jnp.sum(p * dp, axis=0, keepdims=True)
        sg = (p * (dp - centre) * SCALE).astype(jnp.bfloat16)
        att = lax.dot_general(low, v, TN_DIMS, preferred_element_type=jnp.float32)
        dq = lax.dot_general(sg, k, TN_DIMS, preferred_element_type=jnp.float32)
        att_ref[:, lo:lo + HEAD] = att.astype(jnp.bfloat16)
        dq_ref[:, lo:lo + HEAD] = dq.astype(jnp.bfloat16)
        dk = jnp.dot(sg, q, preferred_element_type=jnp.float32)
        dv = jnp.dot(low, g, preferred_element_type=jnp.float32)
        for j in range(SLOTS):
            rows = slice(j * LAT, (j + 1) * LAT)
            acc[dst[j], :, lo:lo + HEAD] += dk[rows]
            acc[dst[j], :, COLS + lo:COLS + lo + HEAD] += dv[rows]

    @pl.when(group == GROUPS - 1)
    def _():
        dkv_ref[...] = acc[...].astype(jnp.bfloat16)


def attention(rel, dst, docs, tok, queries, grad_out, pieces):
    tokens = queries.shape[0]
    block = pl.BlockSpec((GROUP, COLS), lambda g, *_: (g, 0))
    return pl.pallas_call(
        attention_kernel,
        grid_spec=pltpu.PrefetchScalarGridSpec(
            num_scalar_prefetch=3,
            grid=(GROUPS,),
            in_specs=[
                pl.BlockSpec((1, 1, GROUP), lambda g, *_: (g, 0, 0)),
                block,
                block,
            ] + [pl.BlockSpec(memory_space=pl.ANY)] * NX,
            out_specs=[
                block,
                block,
                pl.BlockSpec((IMAGES, LAT, WIDE), lambda g, *_: (0, 0, 0)),
            ],
            scratch_shapes=[
                pltpu.VMEM((IMAGES, LAT, WIDE), jnp.bfloat16),
                pltpu.VMEM((IMAGES, LAT, WIDE), jnp.float32),
                pltpu.SemaphoreType.DMA((NX,)),
            ],
        ),
        out_shape=[
            jax.ShapeDtypeStruct((tokens, COLS), jnp.bfloat16),
            jax.ShapeDtypeStruct((tokens, COLS), jnp.bfloat16),
            jax.ShapeDtypeStruct((IMAGES, LAT, WIDE), jnp.bfloat16),
        ],
        compiler_params=pltpu.CompilerParams(
            dimension_semantics=("arbitrary",), vmem_limit_bytes=40 * 2**20
        ),
        cost_estimate=pl.CostEstimate(
            flops=12 * tokens * GROUP * COLS, bytes_accessed=9 * 2**20, transcendentals=0
        ),
    )(rel, dst, docs, tok, queries, grad_out, *pieces)


def from_offset(value, axis, size, step):
    return lax.ppermute(value, axis, [(i, (i - step) % size) for i in range(size)])


def from_partner(value, axis, size, bit):
    return lax.ppermute(value, axis, [(i, i ^ bit) for i in range(size)])


def gather(value, axis, size):
    copies = jnp.broadcast_to(value[None], (size,) + value.shape)
    return lax.all_to_all(copies, axis, 0, 0, tiled=True)


def local(queries, latents, key_weight, value_weight, grad_out, pairs, image_slot, token_doc):
    x = lax.axis_index("x")
    core = lax.axis_index("core")

    weight = jnp.concatenate([key_weight, value_weight], axis=1)
    weight = gather(weight, ("z", "x"), NZ * NX).reshape(VIS, WIDE)
    kv = jnp.dot(latents[0], weight, preferred_element_type=jnp.float32).astype(jnp.bfloat16)
    column = gather(kv, "z", NZ)
    pieces = [column] + [from_offset(column, "x", NX, i) for i in range(1, NX)]

    matches = pairs[..., None] == jnp.arange(IMAGES, dtype=jnp.int32)
    slot = jnp.sum(jnp.where(matches, image_slot, 0), axis=-1).astype(jnp.int32)
    slot_z, slot_x = slot // NX, slot % NX
    rel = (slot_x - x) % NX * NZ + slot_z
    docs = jnp.where(pairs >= 0, pairs // IPD, -1)
    tok = token_doc.reshape(GROUPS, 1, GROUP)
    attended, grad_queries, dkv = attention(rel, slot, docs, tok, queries, grad_out, pieces)

    dkv = lax.all_to_all(dkv, ("z", "x"), 0, 0, tiled=True)
    dkv = jnp.sum(dkv.astype(jnp.float32), axis=0).astype(jnp.bfloat16)

    term = lax.dot_general(dkv, weight, NT_DIMS, preferred_element_type=jnp.float32)
    half = LAT // 2
    keep = jnp.where(core == 0, term[:half], term[half:])
    give = jnp.where(core == 0, term[half:], term[:half])
    term = keep + from_partner(give, "core", 2, 1)
    term = term + from_partner(term, "y", NY, 1)
    for bit in (2, 4):
        low = term.astype(jnp.bfloat16)
        term = low.astype(jnp.float32) + from_partner(low, "y", NY, bit).astype(jnp.float32)
    term = term.astype(jnp.bfloat16)
    other = from_partner(term, "core", 2, 1)
    first = jnp.where(core == 0, term, other)
    second = jnp.where(core == 0, other, term)
    return attended, grad_queries, jnp.concatenate([first, second])[None]


def solution(mesh):
    fine = Mesh(mesh.devices.reshape(NZ, NX, NY, 2), ("z", "x", "y", "core"))
    seq, tensor = ("z", "x"), ("y", "core")
    in_specs = (
        P(seq, tensor),
        P(seq, None, None),
        P(seq, tensor),
        P(seq, tensor),
        P(seq, tensor),
        P(seq, None),
        P(),
        P(seq),
    )
    out_specs = (P(seq, tensor), P(seq, tensor), P(seq, None, None))
    return jax.shard_map(local, mesh=fine, in_specs=in_specs, out_specs=out_specs, check_vma=False)
```

```python
import jax
import jax.numpy as jnp
from jax import lax
from jax.experimental import pallas as pl
from jax.experimental.pallas import tpu as pltpu
from jax.sharding import Mesh
from jax.sharding import PartitionSpec as P

HEAD = 128
LAT = 64
GROUP = 256
GROUPS = 8
SLOTS = 4
IPD = 4
NX = 4
NZ = 8
NY = 8
WROWS = 40
COLS = 256
WIDE = 2 * COLS
VIS = 1280
IMAGES = 32
MASKED = -1.0e30
SCALE = HEAD ** -0.5
LOG2E = 1.4426950408889634

NT_DIMS = (((1,), (1,)), ((), ()))
TN_DIMS = (((0,), (0,)), ((), ()))


def attention_kernel(src_ref, dst_ref, doc_ref, tok_ref, q_ref, g_ref, kv_ref,
                     att_ref, dq_ref, dkv_ref, kv, acc, sem):
    group = pl.program_id(0)

    @pl.when(group == 0)
    def _():
        copy = pltpu.make_async_copy(kv_ref, kv, sem)
        copy.start()
        acc[...] = jnp.zeros_like(acc)
        copy.wait()

    tok = tok_ref[0]
    src = [src_ref[group, j] for j in range(SLOTS)]
    dst = [dst_ref[group, j] for j in range(SLOTS)]
    bias = [jnp.where(tok == doc_ref[group, j], 0.0, MASKED) for j in range(SLOTS)]
    bias = jnp.concatenate([jnp.broadcast_to(b, (LAT, GROUP)) for b in bias], axis=0)
    heads = [head * HEAD for head in range(COLS // HEAD)]
    keys = [jnp.concatenate([kv[r, :, lo:lo + HEAD] for r in src], axis=0) for lo in heads]
    values = [jnp.concatenate([kv[r, :, COLS + lo:COLS + lo + HEAD] for r in src], axis=0) for lo in heads]
    queries = [q_ref[:, lo:lo + HEAD] for lo in heads]
    grads = [g_ref[:, lo:lo + HEAD] for lo in heads]
    scores = [
        lax.dot_general(k, q, NT_DIMS, preferred_element_type=jnp.float32)
        for k, q in zip(keys, queries)
    ]
    prob_grads = [
        lax.dot_general(v, g, NT_DIMS, preferred_element_type=jnp.float32)
        for v, g in zip(values, grads)
    ]
    lows, score_grads = [], []
    for s, dp in zip(scores, prob_grads):
        s = s + bias
        top = jnp.max(s, axis=0, keepdims=True)
        e = jnp.exp2((s - top) * (SCALE * LOG2E))
        p = e * (1.0 / jnp.sum(e, axis=0, keepdims=True))
        lows.append(p.astype(jnp.bfloat16))
        centre = jnp.sum(p * dp, axis=0, keepdims=True)
        score_grads.append((p * (dp - centre) * SCALE).astype(jnp.bfloat16))
    for i, lo in enumerate(heads):
        att = lax.dot_general(lows[i], values[i], TN_DIMS, preferred_element_type=jnp.float32)
        dq = lax.dot_general(score_grads[i], keys[i], TN_DIMS, preferred_element_type=jnp.float32)
        att_ref[:, lo:lo + HEAD] = att.astype(jnp.bfloat16)
        dq_ref[:, lo:lo + HEAD] = dq.astype(jnp.bfloat16)
        dk = jnp.dot(score_grads[i], queries[i], preferred_element_type=jnp.float32)
        dv = jnp.dot(lows[i], grads[i], preferred_element_type=jnp.float32)
        for j in range(SLOTS):
            rows = slice(j * LAT, (j + 1) * LAT)
            acc[dst[j], :, lo:lo + HEAD] += dk[rows]
            acc[dst[j], :, COLS + lo:COLS + lo + HEAD] += dv[rows]

    @pl.when(group == GROUPS - 1)
    def _():
        dkv_ref[...] = acc[...].astype(jnp.bfloat16)


def attention(src, dst, docs, tok, queries, grad_out, kv):
    tokens = queries.shape[0]
    block = pl.BlockSpec((GROUP, COLS), lambda g, *_: (g, 0))
    return pl.pallas_call(
        attention_kernel,
        grid_spec=pltpu.PrefetchScalarGridSpec(
            num_scalar_prefetch=3,
            grid=(GROUPS,),
            in_specs=[
                pl.BlockSpec((1, 1, GROUP), lambda g, *_: (g, 0, 0)),
                block,
                block,
                pl.BlockSpec(memory_space=pl.ANY),
            ],
            out_specs=[
                block,
                block,
                pl.BlockSpec((IMAGES, LAT, WIDE), lambda g, *_: (0, 0, 0)),
            ],
            scratch_shapes=[
                pltpu.VMEM((IMAGES, LAT, WIDE), jnp.bfloat16),
                pltpu.VMEM((IMAGES, LAT, WIDE), jnp.float32),
                pltpu.SemaphoreType.DMA,
            ],
        ),
        out_shape=[
            jax.ShapeDtypeStruct((tokens, COLS), jnp.bfloat16),
            jax.ShapeDtypeStruct((tokens, COLS), jnp.bfloat16),
            jax.ShapeDtypeStruct((IMAGES, LAT, WIDE), jnp.bfloat16),
        ],
        compiler_params=pltpu.CompilerParams(
            dimension_semantics=("arbitrary",), vmem_limit_bytes=40 * 2**20
        ),
        cost_estimate=pl.CostEstimate(
            flops=12 * tokens * GROUP * COLS, bytes_accessed=9 * 2**20, transcendentals=0
        ),
    )(src, dst, docs, tok, queries, grad_out, kv)


def from_partner(value, axis, size, bit):
    return lax.ppermute(value, axis, [(i, i ^ bit) for i in range(size)])


def gather(value, axis, size):
    copies = jnp.broadcast_to(value[None], (size,) + value.shape)
    return lax.all_to_all(copies, axis, 0, 0, tiled=True)


def local(queries, latents, key_weight, value_weight, grad_out, pairs, image_slot, token_doc):
    core = lax.axis_index("core")

    weight = jnp.concatenate([key_weight, value_weight], axis=1)
    weight = gather(weight, "z", NZ).reshape(NZ * WROWS, WIDE)
    weight = gather(weight, "x", NX).reshape(VIS, WIDE)
    own = latents[0].reshape(LAT, NZ, NX, WROWS).transpose(0, 2, 1, 3).reshape(LAT, VIS)
    kv = jnp.dot(own, weight, preferred_element_type=jnp.float32).astype(jnp.bfloat16)
    kv = gather(gather(kv, "z", NZ), "x", NX).reshape(IMAGES, LAT, WIDE)

    matches = pairs[..., None] == jnp.arange(IMAGES, dtype=jnp.int32)
    slot = jnp.sum(jnp.where(matches, image_slot, 0), axis=-1).astype(jnp.int32)
    place = slot % NX * NZ + slot // NX
    docs = jnp.where(pairs >= 0, pairs // IPD, -1)
    tok = token_doc.reshape(GROUPS, 1, GROUP)
    attended, grad_queries, dkv = attention(place, place, docs, tok, queries, grad_out, kv)

    dkv = lax.all_to_all(dkv.reshape(NX, NZ, LAT, WIDE), "x", 0, 0, tiled=True)
    dkv = jnp.sum(dkv.astype(jnp.float32), axis=0).astype(jnp.bfloat16)
    dkv = lax.all_to_all(dkv, "z", 0, 0, tiled=True)
    dkv = jnp.sum(dkv.astype(jnp.float32), axis=0).astype(jnp.bfloat16)

    ordered = weight.reshape(NX, NZ, WROWS, WIDE).transpose(1, 0, 2, 3).reshape(VIS, WIDE)
    term = lax.dot_general(dkv, ordered, NT_DIMS, preferred_element_type=jnp.float32)
    half = LAT // 2
    keep = jnp.where(core == 0, term[:half], term[half:])
    give = jnp.where(core == 0, term[half:], term[:half])
    term = (keep + from_partner(give, "core", 2, 1)).astype(jnp.bfloat16)
    term = gather(term, "y", NY)
    term = jnp.sum(term.astype(jnp.float32), axis=0).astype(jnp.bfloat16)
    other = from_partner(term, "core", 2, 1)
    first = jnp.where(core == 0, term, other)
    second = jnp.where(core == 0, other, term)
    return attended, grad_queries, jnp.concatenate([first, second])[None]


def solution(mesh):
    fine = Mesh(mesh.devices.reshape(NZ, NX, NY, 2), ("z", "x", "y", "core"))
    seq, tensor = ("z", "x"), ("y", "core")
    in_specs = (
        P(seq, tensor),
        P(seq, None, None),
        P(seq, tensor),
        P(seq, tensor),
        P(seq, tensor),
        P(seq, None),
        P(),
        P(seq),
    )
    out_specs = (P(seq, tensor), P(seq, tensor), P(seq, None, None))
    return jax.shard_map(local, mesh=fine, in_specs=in_specs, out_specs=out_specs, check_vma=False)
```

```python
import jax
import jax.numpy as jnp
from jax import lax
from jax.experimental import pallas as pl
from jax.experimental.pallas import tpu as pltpu
from jax.sharding import Mesh
from jax.sharding import PartitionSpec as P

HEAD = 128
LAT = 64
GROUP = 256
GROUPS = 8
SLOTS = 4
IPD = 4
NX = 4
NZ = 8
NT = 16
COLS = 256
WIDE = 2 * COLS
VIS = 1280
WROWS = 40
IMAGES = 32
DOCS = 8
QUARTER = LAT // NX
SPAN = 3
WINDOW = SPAN * IPD
MASKED = -1.0e30
SCALE = HEAD ** -0.5
LOG2E = 1.4426950408889634

NT_DIMS = (((1,), (1,)), ((), ()))
TN_DIMS = (((0,), (0,)), ((), ()))


def attention_kernel(src_ref, doc_ref, tok_ref, q_ref, g_ref, kv_ref,
                     att_ref, dq_ref, dkv_ref, acc):
    group = pl.program_id(0)

    @pl.when(group == 0)
    def _():
        acc[...] = jnp.zeros_like(acc)

    tok = tok_ref[0]
    src = [src_ref[group, j] for j in range(SLOTS)]
    bias = [jnp.where(tok == doc_ref[group, j], 0.0, MASKED) for j in range(SLOTS)]
    bias = jnp.concatenate([jnp.broadcast_to(b, (LAT, GROUP)) for b in bias], axis=0)
    heads = [head * HEAD for head in range(COLS // HEAD)]

    def rows_of(lo):
        return jnp.concatenate(
            [kv_ref[part, r, :, lo:lo + HEAD] for r in src for part in range(NX)], axis=0
        )

    keys = [rows_of(lo) for lo in heads]
    values = [rows_of(COLS + lo) for lo in heads]
    queries = [q_ref[:, lo:lo + HEAD] for lo in heads]
    grads = [g_ref[:, lo:lo + HEAD] for lo in heads]
    scores = [
        lax.dot_general(k, q, NT_DIMS, preferred_element_type=jnp.float32)
        for k, q in zip(keys, queries)
    ]
    prob_grads = [
        lax.dot_general(v, g, NT_DIMS, preferred_element_type=jnp.float32)
        for v, g in zip(values, grads)
    ]
    lows, score_grads = [], []
    for s, dp in zip(scores, prob_grads):
        s = s + bias
        top = jnp.max(s, axis=0, keepdims=True)
        e = jnp.exp2((s - top) * (SCALE * LOG2E))
        p = e * (1.0 / jnp.sum(e, axis=0, keepdims=True))
        lows.append(p.astype(jnp.bfloat16))
        centre = jnp.sum(p * dp, axis=0, keepdims=True)
        score_grads.append((p * (dp - centre) * SCALE).astype(jnp.bfloat16))
    for i, lo in enumerate(heads):
        att = lax.dot_general(lows[i], values[i], TN_DIMS, preferred_element_type=jnp.float32)
        dq = lax.dot_general(score_grads[i], keys[i], TN_DIMS, preferred_element_type=jnp.float32)
        att_ref[:, lo:lo + HEAD] = att.astype(jnp.bfloat16)
        dq_ref[:, lo:lo + HEAD] = dq.astype(jnp.bfloat16)
        dk = jnp.dot(score_grads[i], queries[i], preferred_element_type=jnp.float32)
        dv = jnp.dot(lows[i], grads[i], preferred_element_type=jnp.float32)
        for j in range(SLOTS):
            rows = slice(j * LAT, (j + 1) * LAT)
            acc[src[j], :, lo:lo + HEAD] += dk[rows]
            acc[src[j], :, COLS + lo:COLS + lo + HEAD] += dv[rows]

    @pl.when(group == GROUPS - 1)
    def _():
        for part in range(NX):
            rows = slice(part * QUARTER, (part + 1) * QUARTER)
            dkv_ref[part] = acc[:, rows, :].astype(jnp.bfloat16)


def attention(src, docs, tok, queries, grad_out, kv):
    tokens = queries.shape[0]
    held = kv.shape[1]
    block = pl.BlockSpec((GROUP, COLS), lambda g, *_: (g, 0))
    whole = pl.BlockSpec((NX, held, QUARTER, WIDE), lambda g, *_: (0, 0, 0, 0))
    return pl.pallas_call(
        attention_kernel,
        grid_spec=pltpu.PrefetchScalarGridSpec(
            num_scalar_prefetch=2,
            grid=(GROUPS,),
            in_specs=[pl.BlockSpec((1, 1, GROUP), lambda g, *_: (g, 0, 0)), block, block, whole],
            out_specs=[block, block, whole],
            scratch_shapes=[pltpu.VMEM((held, LAT, WIDE), jnp.float32)],
        ),
        out_shape=[
            jax.ShapeDtypeStruct((tokens, COLS), jnp.bfloat16),
            jax.ShapeDtypeStruct((tokens, COLS), jnp.bfloat16),
            jax.ShapeDtypeStruct((NX, held, QUARTER, WIDE), jnp.bfloat16),
        ],
        compiler_params=pltpu.CompilerParams(
            dimension_semantics=("arbitrary",), vmem_limit_bytes=40 * 2**20
        ),
        cost_estimate=pl.CostEstimate(
            flops=12 * tokens * GROUP * COLS, bytes_accessed=9 * 2**20, transcendentals=0
        ),
    )(src, docs, tok, queries, grad_out, kv)


def pick_kernel(index_ref, all_ref, out_ref):
    for n in range(NX * WINDOW):
        out_ref[n] = all_ref[index_ref[n]]


def add_kernel(index_ref, parts_ref, out_ref, acc):
    acc[...] = jnp.zeros_like(acc)
    for n in range(NX * WINDOW):
        acc[index_ref[n]] += parts_ref[n].astype(jnp.float32)
    out_ref[...] = acc[...].astype(jnp.bfloat16)


def by_index(kernel, index, operand, count, scratch):
    return pl.pallas_call(
        kernel,
        in_specs=[
            pl.BlockSpec(memory_space=pltpu.SMEM),
            pl.BlockSpec(memory_space=pltpu.VMEM),
        ],
        out_specs=pl.BlockSpec(memory_space=pltpu.VMEM),
        out_shape=jax.ShapeDtypeStruct((count, QUARTER, WIDE), jnp.bfloat16),
        scratch_shapes=scratch,
        compiler_params=pltpu.CompilerParams(vmem_limit_bytes=16 * 2**20),
        cost_estimate=pl.CostEstimate(flops=0, bytes_accessed=2**21, transcendentals=0),
    )(index, operand)


def gather(value, axis, size):
    copies = jnp.broadcast_to(value[None], (size,) + value.shape)
    return lax.all_to_all(copies, axis, 0, 0, tiled=True)


def lookup(slot_table, image_ids):
    matches = image_ids[..., None] == jnp.arange(IMAGES, dtype=jnp.int32)
    return jnp.sum(jnp.where(matches, slot_table, 0), axis=-1).astype(jnp.int32)


def local(queries, latents, key_weight, value_weight, grad_out, pairs, image_slot, token_doc):
    z = lax.axis_index("z")
    low_doc, high_doc = jnp.min(token_doc), jnp.max(token_doc)
    start = jnp.minimum(low_doc, DOCS - SPAN)
    note = jnp.stack([start, high_doc - start + 1]).astype(jnp.bfloat16)

    weight = jnp.concatenate([key_weight, value_weight], axis=1)
    extra = jnp.broadcast_to(jnp.tile(note, COLS)[None], (8, WIDE))
    column = gather(jnp.concatenate([weight, extra]), "z", NZ)
    notes = column[:, WROWS, :2].reshape(2 * NZ)
    column = column[:, :WROWS].reshape(NZ * WROWS, WIDE)

    own = latents[0].reshape(LAT, NZ, NX, WROWS).transpose(0, 2, 1, 3).reshape(NX, QUARTER, VIS)
    notes = jnp.broadcast_to(jnp.tile(notes, COLS // (2 * NZ)), (NX, QUARTER, COLS))
    own = jnp.concatenate([own, notes], axis=2)
    sent = [jnp.broadcast_to(column[None], (NX,) + column.shape)]
    sent += [own[:, :, i * WIDE:(i + 1) * WIDE] for i in range(3)]
    row = lax.all_to_all(jnp.concatenate(sent, axis=1), "x", 0, 0, tiled=True)
    tall = NZ * WROWS
    weight = row[:, :tall].reshape(VIS, WIDE)
    images = [row[:, tall + i * QUARTER:tall + (i + 1) * QUARTER] for i in range(3)]
    images = jnp.concatenate(images, axis=2).reshape(LAT, 3 * WIDE)
    notes = row[:, tall + 2 * QUARTER, COLS:COLS + 2 * NZ].reshape(NX, NZ, 2).astype(jnp.int32)

    kv = jnp.dot(images[:, :VIS], weight, preferred_element_type=jnp.float32).astype(jnp.bfloat16)
    kv = gather(kv, "z", NZ).reshape(IMAGES, QUARTER, WIDE)

    docs = jnp.where(pairs >= 0, pairs // IPD, -1)
    tok = token_doc.reshape(GROUPS, 1, GROUP)
    starts = lax.dynamic_index_in_dim(notes[:, :, 0], z, axis=1, keepdims=False)
    wanted = starts[:, None] * IPD + jnp.arange(WINDOW, dtype=jnp.int32)
    wanted = lookup(image_slot, wanted).reshape(NX * WINDOW)

    def narrow():
        picked = by_index(pick_kernel, wanted, kv, NX * WINDOW, [])
        held = lax.all_to_all(picked.reshape(NX, WINDOW, QUARTER, WIDE), "x", 0, 0, tiled=True)
        src = jnp.clip(pairs - start * IPD, 0, WINDOW - 1)
        att, dq, dkv = attention(src, docs, tok, queries, grad_out, held)
        dkv = lax.all_to_all(dkv, "x", 0, 0, tiled=True).reshape(NX * WINDOW, QUARTER, WIDE)
        total = pltpu.VMEM((IMAGES, QUARTER, WIDE), jnp.float32)
        return att, dq, by_index(add_kernel, wanted, dkv, IMAGES, [total])

    def full():
        held = gather(kv, "x", NX)
        att, dq, dkv = attention(lookup(image_slot, pairs), docs, tok, queries, grad_out, held)
        dkv = lax.all_to_all(dkv, "x", 0, 0, tiled=True)
        return att, dq, jnp.sum(dkv.astype(jnp.float32), axis=0).astype(jnp.bfloat16)

    attended, grad_queries, dkv = lax.cond(jnp.max(notes[:, :, 1]) <= SPAN, narrow, full)

    dkv = lax.all_to_all(dkv, ("z", "x"), 0, 0, tiled=True).reshape(NZ, LAT, WIDE)
    dkv = jnp.sum(dkv.astype(jnp.float32), axis=0).astype(jnp.bfloat16)

    ordered = weight.reshape(NX, NZ, WROWS, WIDE).transpose(1, 0, 2, 3).reshape(VIS, WIDE)
    term = lax.dot_general(dkv, ordered, NT_DIMS, preferred_element_type=jnp.float32)
    term = term.astype(jnp.bfloat16).reshape(NT, LAT // NT, VIS)
    term = lax.all_to_all(term, ("y", "core"), 0, 0, tiled=True)
    term = jnp.sum(term.astype(jnp.float32), axis=0).astype(jnp.bfloat16)
    term = gather(term, ("y", "core"), NT).reshape(1, LAT, VIS)
    return attended, grad_queries, term


def solution(mesh):
    fine = Mesh(mesh.devices.reshape(NZ, NX, NT // 2, 2), ("z", "x", "y", "core"))
    seq, tensor = ("z", "x"), ("y", "core")
    in_specs = (
        P(seq, tensor),
        P(seq, None, None),
        P(seq, tensor),
        P(seq, tensor),
        P(seq, tensor),
        P(seq, None),
        P(),
        P(seq),
    )
    out_specs = (P(seq, tensor), P(seq, tensor), P(seq, None, None))
    return jax.shard_map(local, mesh=fine, in_specs=in_specs, out_specs=out_specs, check_vma=False)
```

```python
import jax
import jax.numpy as jnp
from jax import lax
from jax.experimental import pallas as pl
from jax.experimental.pallas import tpu as pltpu
from jax.sharding import Mesh
from jax.sharding import PartitionSpec as P

HEAD = 128
LAT = 64
GROUP = 256
GROUPS = 8
BATCH = 2
SLOTS = 4
IPD = 4
NX = 4
NZ = 8
NT = 16
COLS = 256
WIDE = 2 * COLS
VIS = 1280
WROWS = 40
IMAGES = 32
TOKENS = 2048
DOCS = 8
QUARTER = LAT // NX
SPAN = 3
WINDOW = SPAN * IPD
MASKED = -1.0e30
SCALE = HEAD ** -0.5
LOG2E = 1.4426950408889634

NT_DIMS = (((1,), (1,)), ((), ()))
TN_DIMS = (((0,), (0,)), ((), ()))


def attention_kernel(src_ref, doc_ref, tok_ref, q_ref, g_ref, kv_ref,
                     att_ref, dq_ref, dkv_ref, acc):
    step = pl.program_id(0)

    @pl.when(step == 0)
    def _():
        acc[...] = jnp.zeros_like(acc)

    src = [[src_ref[step * BATCH + i, j] for j in range(SLOTS)] for i in range(BATCH)]
    bias = [
        [jnp.where(tok_ref[i] == doc_ref[step * BATCH + i, j], 0.0, MASKED) for j in range(SLOTS)]
        for i in range(BATCH)
    ]
    units = [(i, head * HEAD) for i in range(BATCH) for head in range(COLS // HEAD)]
    tokens = [slice(i * GROUP, (i + 1) * GROUP) for i in range(BATCH)]
    of_slot = [slice(j * LAT, (j + 1) * LAT) for j in range(SLOTS)]

    def rows_of(i, lo):
        return jnp.concatenate(
            [kv_ref[part, r, :, lo:lo + HEAD] for r in src[i] for part in range(NX)], axis=0
        )

    keys = [rows_of(i, lo) for i, lo in units]
    values = [rows_of(i, COLS + lo) for i, lo in units]
    queries = [q_ref[tokens[i], lo:lo + HEAD] for i, lo in units]
    grads = [g_ref[tokens[i], lo:lo + HEAD] for i, lo in units]
    scores = [
        lax.dot_general(k, q, NT_DIMS, preferred_element_type=jnp.float32)
        for k, q in zip(keys, queries)
    ]
    prob_grads = [
        lax.dot_general(v, g, NT_DIMS, preferred_element_type=jnp.float32)
        for v, g in zip(values, grads)
    ]
    lows, score_grads = [], []
    for (i, _), s, dp in zip(units, scores, prob_grads):
        s = jnp.concatenate([s[of_slot[j]] + bias[i][j] for j in range(SLOTS)], axis=0)
        top = jnp.max(s, axis=0, keepdims=True)
        e = jnp.exp2((s - top) * (SCALE * LOG2E))
        inverse = 1.0 / jnp.sum(e, axis=0, keepdims=True)
        centre = jnp.sum(e * dp, axis=0, keepdims=True) * inverse
        p = e * inverse
        lows.append(p.astype(jnp.bfloat16))
        score_grads.append((p * (dp - centre) * SCALE).astype(jnp.bfloat16))
    for u, (i, lo) in enumerate(units):
        att = lax.dot_general(lows[u], values[u], TN_DIMS, preferred_element_type=jnp.float32)
        dq = lax.dot_general(score_grads[u], keys[u], TN_DIMS, preferred_element_type=jnp.float32)
        att_ref[tokens[i], lo:lo + HEAD] = att.astype(jnp.bfloat16)
        dq_ref[tokens[i], lo:lo + HEAD] = dq.astype(jnp.bfloat16)
        dk = jnp.dot(score_grads[u], queries[u], preferred_element_type=jnp.float32)
        dv = jnp.dot(lows[u], grads[u], preferred_element_type=jnp.float32)
        for j in range(SLOTS):
            acc[src[i][j], :, lo:lo + HEAD] += dk[of_slot[j]]
            acc[src[i][j], :, COLS + lo:COLS + lo + HEAD] += dv[of_slot[j]]

    @pl.when(step == GROUPS // BATCH - 1)
    def _():
        for part in range(NX):
            rows = slice(part * QUARTER, (part + 1) * QUARTER)
            dkv_ref[part] = acc[:, rows, :].astype(jnp.bfloat16)


def attention(src, docs, tok, queries, grad_out, kv):
    tokens = queries.shape[0]
    held = kv.shape[1]
    block = pl.BlockSpec((BATCH * GROUP, COLS), lambda g, *_: (g, 0))
    whole = pl.BlockSpec((NX, held, QUARTER, WIDE), lambda g, *_: (0, 0, 0, 0))
    return pl.pallas_call(
        attention_kernel,
        grid_spec=pltpu.PrefetchScalarGridSpec(
            num_scalar_prefetch=2,
            grid=(GROUPS // BATCH,),
            in_specs=[pl.BlockSpec((BATCH, 1, GROUP), lambda g, *_: (g, 0, 0)), block, block, whole],
            out_specs=[block, block, whole],
            scratch_shapes=[pltpu.VMEM((held, LAT, WIDE), jnp.float32)],
        ),
        out_shape=[
            jax.ShapeDtypeStruct((tokens, COLS), jnp.bfloat16),
            jax.ShapeDtypeStruct((tokens, COLS), jnp.bfloat16),
            jax.ShapeDtypeStruct((NX, held, QUARTER, WIDE), jnp.bfloat16),
        ],
        compiler_params=pltpu.CompilerParams(
            dimension_semantics=("arbitrary",), vmem_limit_bytes=40 * 2**20
        ),
        cost_estimate=pl.CostEstimate(
            flops=12 * tokens * GROUP * COLS, bytes_accessed=9 * 2**20, transcendentals=0
        ),
    )(src, docs, tok, queries, grad_out, kv)


def pick_kernel(index_ref, all_ref, out_ref):
    for n in range(NX * WINDOW):
        out_ref[n] = all_ref[index_ref[n]]


def add_kernel(index_ref, parts_ref, out_ref, acc):
    acc[...] = jnp.zeros_like(acc)
    for n in range(NX * WINDOW):
        acc[index_ref[n]] += parts_ref[n].astype(jnp.float32)
    out_ref[...] = acc[...].astype(jnp.bfloat16)


def by_index(kernel, index, operand, count, scratch):
    return pl.pallas_call(
        kernel,
        in_specs=[
            pl.BlockSpec(memory_space=pltpu.SMEM),
            pl.BlockSpec(memory_space=pltpu.VMEM),
        ],
        out_specs=pl.BlockSpec(memory_space=pltpu.VMEM),
        out_shape=jax.ShapeDtypeStruct((count, QUARTER, WIDE), jnp.bfloat16),
        scratch_shapes=scratch,
        compiler_params=pltpu.CompilerParams(vmem_limit_bytes=16 * 2**20),
        cost_estimate=pl.CostEstimate(flops=0, bytes_accessed=2**21, transcendentals=0),
    )(index, operand)


def gather(value, axis, size):
    copies = jnp.broadcast_to(value[None], (size,) + value.shape)
    return lax.all_to_all(copies, axis, 0, 0, tiled=True)


def lookup(slot_table, image_ids):
    matches = image_ids[..., None] == jnp.arange(IMAGES, dtype=jnp.int32)
    return jnp.sum(jnp.where(matches, slot_table, 0), axis=-1).astype(jnp.int32)


def local(queries, latents, key_weight, value_weight, grad_out, pairs, image_slot, token_doc):
    z = lax.axis_index("z")

    tok = token_doc.reshape(TOKENS // WIDE, WIDE)
    note = jnp.stack([jnp.min(tok, axis=0), jnp.max(tok, axis=0)]).astype(jnp.bfloat16)
    weight = jnp.concatenate([key_weight, value_weight], axis=1)
    column = jnp.concatenate([weight, jnp.pad(note, ((0, 6), (0, 0)))])
    column = gather(column, "z", NZ)
    notes = column[:, WROWS:WROWS + 2].reshape(2 * NZ, WIDE)

    column = column[:, :WROWS].reshape(NZ * WROWS, WIDE)
    row = gather(jnp.concatenate([column, notes]), "x", NX)
    weight = row[:, :NZ * WROWS].reshape(VIS, WIDE)
    notes = row[:, NZ * WROWS:].reshape(NX, NZ, 2, WIDE)
    low_doc = jnp.min(notes[:, :, 0], axis=-1).astype(jnp.int32)
    high_doc = jnp.max(notes[:, :, 1], axis=-1).astype(jnp.int32)
    starts = jnp.minimum(low_doc, DOCS - SPAN)
    fits = jnp.max(high_doc - starts) < SPAN

    own = latents[0].reshape(LAT, NZ, NX, WROWS).transpose(0, 2, 1, 3).reshape(LAT, VIS)
    kv = jnp.dot(own, weight, preferred_element_type=jnp.float32).astype(jnp.bfloat16)
    kv = jnp.broadcast_to(kv.reshape(1, NX, QUARTER, WIDE), (NZ, NX, QUARTER, WIDE))
    kv = lax.all_to_all(kv.reshape(IMAGES, QUARTER, WIDE), ("z", "x"), 0, 0, tiled=True)

    docs = jnp.where(pairs >= 0, pairs // IPD, -1)
    tok = token_doc.reshape(GROUPS, 1, GROUP)
    starts = lax.dynamic_index_in_dim(starts, z, axis=1, keepdims=False)
    start = lax.dynamic_index_in_dim(starts, lax.axis_index("x"), keepdims=False)
    wanted = starts[:, None] * IPD + jnp.arange(WINDOW, dtype=jnp.int32)
    wanted = lookup(image_slot, wanted).reshape(NX * WINDOW)

    def narrow():
        picked = by_index(pick_kernel, wanted, kv, NX * WINDOW, [])
        held = lax.all_to_all(picked.reshape(NX, WINDOW, QUARTER, WIDE), "x", 0, 0, tiled=True)
        src = jnp.clip(pairs - start * IPD, 0, WINDOW - 1)
        att, dq, dkv = attention(src, docs, tok, queries, grad_out, held)
        dkv = lax.all_to_all(dkv, "x", 0, 0, tiled=True).reshape(NX * WINDOW, QUARTER, WIDE)
        total = pltpu.VMEM((IMAGES, QUARTER, WIDE), jnp.float32)
        return att, dq, by_index(add_kernel, wanted, dkv, IMAGES, [total])

    def full():
        held = gather(kv, "x", NX)
        att, dq, dkv = attention(lookup(image_slot, pairs), docs, tok, queries, grad_out, held)
        dkv = lax.all_to_all(dkv, "x", 0, 0, tiled=True)
        return att, dq, jnp.sum(dkv.astype(jnp.float32), axis=0).astype(jnp.bfloat16)

    attended, grad_queries, dkv = lax.cond(fits, narrow, full)

    dkv = lax.all_to_all(dkv, ("z", "x"), 0, 0, tiled=True).reshape(NZ, LAT, WIDE)
    dkv = jnp.sum(dkv.astype(jnp.float32), axis=0).astype(jnp.bfloat16)

    ordered = weight.reshape(NX, NZ, WROWS, WIDE).transpose(1, 0, 2, 3).reshape(VIS, WIDE)
    term = lax.dot_general(dkv, ordered, NT_DIMS, preferred_element_type=jnp.float32)
    term = term.astype(jnp.bfloat16).reshape(NT, LAT // NT, VIS)
    term = lax.all_to_all(term, ("y", "core"), 0, 0, tiled=True)
    term = jnp.sum(term.astype(jnp.float32), axis=0).astype(jnp.bfloat16)
    term = gather(term, ("y", "core"), NT).reshape(1, LAT, VIS)
    return attended, grad_queries, term


def solution(mesh):
    fine = Mesh(mesh.devices.reshape(NZ, NX, NT // 2, 2), ("z", "x", "y", "core"))
    seq, tensor = ("z", "x"), ("y", "core")
    in_specs = (
        P(seq, tensor),
        P(seq, None, None),
        P(seq, tensor),
        P(seq, tensor),
        P(seq, tensor),
        P(seq, None),
        P(),
        P(seq),
    )
    out_specs = (P(seq, tensor), P(seq, tensor), P(seq, None, None))
    return jax.shard_map(local, mesh=fine, in_specs=in_specs, out_specs=out_specs, check_vma=False)
```

```python
import jax
import jax.numpy as jnp
from jax import lax
from jax.experimental import pallas as pl
from jax.experimental.pallas import tpu as pltpu
from jax.sharding import Mesh
from jax.sharding import PartitionSpec as P

HEAD = 128
LAT = 64
GROUP = 256
GROUPS = 8
BATCH = 2
HEADS = 2
SLOTS = 4
IPD = 4
NX = 4
NZ = 8
NT = 16
COLS = 256
WIDE = 2 * COLS
VIS = 1280
WROWS = 40
IMAGES = 32
TOKENS = 2048
DOCS = 8
QUARTER = LAT // NX
SPAN = 3
WINDOW = SPAN * IPD
MASKED = -1.0e30
SCALE = HEAD ** -0.5
LOG2E = 1.4426950408889634

NT_DIMS = (((1,), (1,)), ((), ()))
TN_DIMS = (((0,), (0,)), ((), ()))


def rows_of(kv_ref, places, lo):
    return jnp.concatenate(
        [kv_ref[part, r, :, lo:lo + HEAD] for r in places for part in range(NX)], axis=0
    )


def attention_kernel(src_ref, doc_ref, tok_ref, q_ref, g_ref, kv_ref,
                     low_ref, sg_ref, dkv_ref, acc):
    step = pl.program_id(0)

    @pl.when(step == 0)
    def _():
        acc[...] = jnp.zeros_like(acc)

    src = [[src_ref[step * BATCH + i, j] for j in range(SLOTS)] for i in range(BATCH)]
    bias = [
        [jnp.where(tok_ref[i] == doc_ref[step * BATCH + i, j], 0.0, MASKED) for j in range(SLOTS)]
        for i in range(BATCH)
    ]
    units = [(i, head * HEAD) for i in range(BATCH) for head in range(COLS // HEAD)]
    tokens = [slice(i * GROUP, (i + 1) * GROUP) for i in range(BATCH)]
    of_slot = [slice(j * LAT, (j + 1) * LAT) for j in range(SLOTS)]

    keys = [rows_of(kv_ref, src[i], lo) for i, lo in units]
    values = [rows_of(kv_ref, src[i], COLS + lo) for i, lo in units]
    queries = [q_ref[tokens[i], lo:lo + HEAD] for i, lo in units]
    grads = [g_ref[tokens[i], lo:lo + HEAD] for i, lo in units]
    scores = [
        lax.dot_general(k, q, NT_DIMS, preferred_element_type=jnp.float32)
        for k, q in zip(keys, queries)
    ]
    prob_grads = [
        lax.dot_general(v, g, NT_DIMS, preferred_element_type=jnp.float32)
        for v, g in zip(values, grads)
    ]
    lows, score_grads = [], []
    for (i, _), s, dp in zip(units, scores, prob_grads):
        s = jnp.concatenate([s[of_slot[j]] + bias[i][j] for j in range(SLOTS)], axis=0)
        top = jnp.max(s, axis=0, keepdims=True)
        e = jnp.exp2((s - top) * (SCALE * LOG2E))
        inverse = 1.0 / jnp.sum(e, axis=0, keepdims=True)
        centre = jnp.sum(e * dp, axis=0, keepdims=True) * inverse
        p = e * inverse
        lows.append(p.astype(jnp.bfloat16))
        score_grads.append((p * (dp - centre) * SCALE).astype(jnp.bfloat16))
    for u, (i, lo) in enumerate(units):
        low_ref[i, lo // HEAD] = lows[u]
        sg_ref[i, lo // HEAD] = score_grads[u]
        dk = jnp.dot(score_grads[u], queries[u], preferred_element_type=jnp.float32)
        dv = jnp.dot(lows[u], grads[u], preferred_element_type=jnp.float32)
        for j in range(SLOTS):
            acc[src[i][j], :, lo:lo + HEAD] += dk[of_slot[j]]
            acc[src[i][j], :, COLS + lo:COLS + lo + HEAD] += dv[of_slot[j]]

    @pl.when(step == GROUPS // BATCH - 1)
    def _():
        for part in range(NX):
            rows = slice(part * QUARTER, (part + 1) * QUARTER)
            dkv_ref[part] = acc[:, rows, :].astype(jnp.bfloat16)


def output_kernel(src_ref, low_ref, sg_ref, kv_ref, att_ref, dq_ref):
    step = pl.program_id(0)
    for i in range(BATCH):
        src = [src_ref[step * BATCH + i, j] for j in range(SLOTS)]
        rows = slice(i * GROUP, (i + 1) * GROUP)
        for head in range(HEADS):
            lo = head * HEAD
            keys = rows_of(kv_ref, src, lo)
            values = rows_of(kv_ref, src, COLS + lo)
            att = lax.dot_general(low_ref[i, head], values, TN_DIMS, preferred_element_type=jnp.float32)
            dq = lax.dot_general(sg_ref[i, head], keys, TN_DIMS, preferred_element_type=jnp.float32)
            att_ref[rows, lo:lo + HEAD] = att.astype(jnp.bfloat16)
            dq_ref[rows, lo:lo + HEAD] = dq.astype(jnp.bfloat16)


def blocks(held):
    tokens = pl.BlockSpec((BATCH * GROUP, COLS), lambda g, *_: (g, 0))
    square = pl.BlockSpec((BATCH, HEADS, SLOTS * LAT, GROUP), lambda g, *_: (g, 0, 0, 0))
    whole = pl.BlockSpec((NX, held, QUARTER, WIDE), lambda g, *_: (0, 0, 0, 0))
    return tokens, square, whole


PARAMS = pltpu.CompilerParams(
    dimension_semantics=("arbitrary",), vmem_limit_bytes=40 * 2**20
)


def attention(src, docs, tok, queries, grad_out, kv):
    held = kv.shape[1]
    tokens, square, whole = blocks(held)
    weights = jax.ShapeDtypeStruct((GROUPS, HEADS, SLOTS * LAT, GROUP), jnp.bfloat16)
    return pl.pallas_call(
        attention_kernel,
        grid_spec=pltpu.PrefetchScalarGridSpec(
            num_scalar_prefetch=2,
            grid=(GROUPS // BATCH,),
            in_specs=[pl.BlockSpec((BATCH, 1, GROUP), lambda g, *_: (g, 0, 0)), tokens, tokens, whole],
            out_specs=[square, square, whole],
            scratch_shapes=[pltpu.VMEM((held, LAT, WIDE), jnp.float32)],
        ),
        out_shape=[weights, weights, jax.ShapeDtypeStruct(kv.shape, jnp.bfloat16)],
        compiler_params=PARAMS,
        cost_estimate=pl.CostEstimate(
            flops=8 * TOKENS * GROUP * COLS, bytes_accessed=9 * 2**20, transcendentals=0
        ),
    )(src, docs, tok, queries, grad_out, kv)


def outputs(src, low, score_grad, kv):
    tokens, square, whole = blocks(kv.shape[1])
    out = jax.ShapeDtypeStruct((TOKENS, COLS), jnp.bfloat16)
    return pl.pallas_call(
        output_kernel,
        grid_spec=pltpu.PrefetchScalarGridSpec(
            num_scalar_prefetch=1,
            grid=(GROUPS // BATCH,),
            in_specs=[square, square, whole],
            out_specs=[tokens, tokens],
        ),
        out_shape=[out, out],
        compiler_params=PARAMS,
        cost_estimate=pl.CostEstimate(
            flops=4 * TOKENS * GROUP * COLS, bytes_accessed=8 * 2**20, transcendentals=0
        ),
    )(src, low, score_grad, kv)


def pick_kernel(index_ref, all_ref, out_ref):
    for n in range(NX * WINDOW):
        out_ref[n] = all_ref[index_ref[n]]


def add_kernel(index_ref, parts_ref, out_ref, acc):
    acc[...] = jnp.zeros_like(acc)
    for n in range(NX * WINDOW):
        acc[index_ref[n]] += parts_ref[n].astype(jnp.float32)
    out_ref[...] = acc[...].astype(jnp.bfloat16)


def by_index(kernel, index, operand, count, scratch):
    return pl.pallas_call(
        kernel,
        in_specs=[
            pl.BlockSpec(memory_space=pltpu.SMEM),
            pl.BlockSpec(memory_space=pltpu.VMEM),
        ],
        out_specs=pl.BlockSpec(memory_space=pltpu.VMEM),
        out_shape=jax.ShapeDtypeStruct((count, QUARTER, WIDE), jnp.bfloat16),
        scratch_shapes=scratch,
        compiler_params=pltpu.CompilerParams(vmem_limit_bytes=16 * 2**20),
        cost_estimate=pl.CostEstimate(flops=0, bytes_accessed=2**21, transcendentals=0),
    )(index, operand)


def gather(value, axis, size):
    copies = jnp.broadcast_to(value[None], (size,) + value.shape)
    return lax.all_to_all(copies, axis, 0, 0, tiled=True)


def lookup(slot_table, image_ids):
    matches = image_ids[..., None] == jnp.arange(IMAGES, dtype=jnp.int32)
    return jnp.sum(jnp.where(matches, slot_table, 0), axis=-1).astype(jnp.int32)


def local(queries, latents, key_weight, value_weight, grad_out, pairs, image_slot, token_doc):
    weight = jnp.concatenate([key_weight, value_weight], axis=1)
    column = gather(weight, "z", NZ).reshape(NZ * WROWS, WIDE)

    tok = token_doc.reshape(TOKENS // WIDE, WIDE)
    note = jnp.stack([jnp.min(tok, axis=0), jnp.max(tok, axis=0)]).astype(jnp.bfloat16)
    row = gather(jnp.concatenate([column, jnp.pad(note, ((0, 6), (0, 0)))]), "x", NX)
    weight = row[:, :NZ * WROWS].reshape(VIS, WIDE)
    notes = row[:, NZ * WROWS:NZ * WROWS + 2]
    starts = jnp.minimum(jnp.min(notes[:, 0], axis=-1).astype(jnp.int32), DOCS - SPAN)
    fits = jnp.max(jnp.max(notes[:, 1], axis=-1).astype(jnp.int32) - starts) < SPAN

    own = latents[0].reshape(LAT, NZ, NX, WROWS).transpose(0, 2, 1, 3).reshape(LAT, VIS)
    kv = jnp.dot(own, weight, preferred_element_type=jnp.float32).astype(jnp.bfloat16)
    kv = jnp.broadcast_to(kv.reshape(1, NX, QUARTER, WIDE), (NZ, NX, QUARTER, WIDE))
    kv = lax.all_to_all(kv.reshape(IMAGES, QUARTER, WIDE), ("z", "x"), 0, 0, tiled=True)

    docs = jnp.where(pairs >= 0, pairs // IPD, -1)
    tok = token_doc.reshape(GROUPS, 1, GROUP)
    start = lax.dynamic_index_in_dim(starts, lax.axis_index("x"), keepdims=False)
    wanted = starts[:, None] * IPD + jnp.arange(WINDOW, dtype=jnp.int32)
    wanted = lookup(image_slot, wanted).reshape(NX * WINDOW)

    def narrow():
        picked = by_index(pick_kernel, wanted, kv, NX * WINDOW, [])
        held = lax.all_to_all(picked.reshape(NX, WINDOW, QUARTER, WIDE), "x", 0, 0, tiled=True)
        src = jnp.clip(pairs - start * IPD, 0, WINDOW - 1)
        low, score_grad, dkv = attention(src, docs, tok, queries, grad_out, held)
        dkv = lax.all_to_all(dkv, "x", 0, 0, tiled=True).reshape(NX * WINDOW, QUARTER, WIDE)
        att, dq = outputs(src, low, score_grad, held)
        total = pltpu.VMEM((IMAGES, QUARTER, WIDE), jnp.float32)
        return att, dq, by_index(add_kernel, wanted, dkv, IMAGES, [total])

    def full():
        held = gather(kv, "x", NX)
        src = lookup(image_slot, pairs)
        low, score_grad, dkv = attention(src, docs, tok, queries, grad_out, held)
        att, dq = outputs(src, low, score_grad, held)
        dkv = lax.all_to_all(dkv, "x", 0, 0, tiled=True)
        return att, dq, jnp.sum(dkv.astype(jnp.float32), axis=0).astype(jnp.bfloat16)

    attended, grad_queries, dkv = lax.cond(fits, narrow, full)

    dkv = lax.all_to_all(dkv, ("z", "x"), 0, 0, tiled=True).reshape(NZ, LAT, WIDE)
    dkv = jnp.sum(dkv.astype(jnp.float32), axis=0).astype(jnp.bfloat16)

    ordered = weight.reshape(NX, NZ, WROWS, WIDE).transpose(1, 0, 2, 3).reshape(VIS, WIDE)
    term = lax.dot_general(dkv, ordered, NT_DIMS, preferred_element_type=jnp.float32)
    term = term.astype(jnp.bfloat16).reshape(NT, LAT // NT, VIS)
    term = lax.all_to_all(term, ("y", "core"), 0, 0, tiled=True)
    term = jnp.sum(term.astype(jnp.float32), axis=0).astype(jnp.bfloat16)
    term = gather(term, ("y", "core"), NT).reshape(1, LAT, VIS)
    return attended, grad_queries, term


def solution(mesh):
    fine = Mesh(mesh.devices.reshape(NZ, NX, NT // 2, 2), ("z", "x", "y", "core"))
    seq, tensor = ("z", "x"), ("y", "core")
    in_specs = (
        P(seq, tensor),
        P(seq, None, None),
        P(seq, tensor),
        P(seq, tensor),
        P(seq, tensor),
        P(seq, None),
        P(),
        P(seq),
    )
    out_specs = (P(seq, tensor), P(seq, tensor), P(seq, None, None))
    return jax.shard_map(local, mesh=fine, in_specs=in_specs, out_specs=out_specs, check_vma=False)
```

```python
import jax
import jax.numpy as jnp
from jax import lax
from jax.experimental import pallas as pl
from jax.experimental.pallas import tpu as pltpu
from jax.sharding import Mesh
from jax.sharding import PartitionSpec as P

HEAD = 128
LAT = 64
GROUP = 256
GROUPS = 8
BATCH = 4
HEADS = 2
SLOTS = 4
IPD = 4
NX = 4
NZ = 8
NT = 16
COLS = 256
WIDE = 2 * COLS
VIS = 1280
WROWS = 40
IMAGES = 32
TOKENS = 2048
DOCS = 8
QUARTER = LAT // NX
SPAN = 3
WINDOW = SPAN * IPD
MASKED = -1.0e30
SCALE = HEAD ** -0.5
LOG2E = 1.4426950408889634

NT_DIMS = (((1,), (1,)), ((), ()))
TN_DIMS = (((0,), (0,)), ((), ()))


def rows_of(kv_ref, places, lo):
    return jnp.concatenate(
        [kv_ref[part, r, :, lo:lo + HEAD] for r in places for part in range(NX)], axis=0
    )


def attention_kernel(src_ref, doc_ref, tok_ref, q_ref, g_ref, kv_ref,
                     low_ref, sg_ref, dkv_ref, acc):
    step = pl.program_id(0)

    @pl.when(step == 0)
    def _():
        acc[...] = jnp.zeros_like(acc)

    src = [[src_ref[step * BATCH + i, j] for j in range(SLOTS)] for i in range(BATCH)]
    bias = [
        [jnp.where(tok_ref[i] == doc_ref[step * BATCH + i, j], 0.0, MASKED) for j in range(SLOTS)]
        for i in range(BATCH)
    ]
    units = [(i, head * HEAD) for i in range(BATCH) for head in range(COLS // HEAD)]
    tokens = [slice(i * GROUP, (i + 1) * GROUP) for i in range(BATCH)]
    of_slot = [slice(j * LAT, (j + 1) * LAT) for j in range(SLOTS)]

    keys = [rows_of(kv_ref, src[i], lo) for i, lo in units]
    values = [rows_of(kv_ref, src[i], COLS + lo) for i, lo in units]
    queries = [q_ref[tokens[i], lo:lo + HEAD] for i, lo in units]
    grads = [g_ref[tokens[i], lo:lo + HEAD] for i, lo in units]
    scores = [
        lax.dot_general(k, q, NT_DIMS, preferred_element_type=jnp.float32)
        for k, q in zip(keys, queries)
    ]
    prob_grads = [
        lax.dot_general(v, g, NT_DIMS, preferred_element_type=jnp.float32)
        for v, g in zip(values, grads)
    ]
    lows, score_grads = [], []
    for (i, _), s, dp in zip(units, scores, prob_grads):
        s = jnp.concatenate([s[of_slot[j]] + bias[i][j] for j in range(SLOTS)], axis=0)
        top = jnp.max(s, axis=0, keepdims=True)
        e = jnp.exp2((s - top) * (SCALE * LOG2E))
        inverse = 1.0 / jnp.sum(e, axis=0, keepdims=True)
        centre = jnp.sum(e * dp, axis=0, keepdims=True) * inverse
        p = e * inverse
        lows.append(p.astype(jnp.bfloat16))
        score_grads.append((p * (dp - centre) * SCALE).astype(jnp.bfloat16))
    for u, (i, lo) in enumerate(units):
        low_ref[i, lo // HEAD] = lows[u]
        sg_ref[i, lo // HEAD] = score_grads[u]
        dk = jnp.dot(score_grads[u], queries[u], preferred_element_type=jnp.float32)
        dv = jnp.dot(lows[u], grads[u], preferred_element_type=jnp.float32)
        for j in range(SLOTS):
            acc[src[i][j], :, lo:lo + HEAD] += dk[of_slot[j]]
            acc[src[i][j], :, COLS + lo:COLS + lo + HEAD] += dv[of_slot[j]]

    @pl.when(step == GROUPS // BATCH - 1)
    def _():
        for part in range(NX):
            rows = slice(part * QUARTER, (part + 1) * QUARTER)
            dkv_ref[part] = acc[:, rows, :].astype(jnp.bfloat16)


def output_kernel(src_ref, low_ref, sg_ref, kv_ref, att_ref, dq_ref):
    step = pl.program_id(0)
    for i in range(BATCH):
        src = [src_ref[step * BATCH + i, j] for j in range(SLOTS)]
        rows = slice(i * GROUP, (i + 1) * GROUP)
        for head in range(HEADS):
            lo = head * HEAD
            keys = rows_of(kv_ref, src, lo)
            values = rows_of(kv_ref, src, COLS + lo)
            att = lax.dot_general(low_ref[i, head], values, TN_DIMS, preferred_element_type=jnp.float32)
            dq = lax.dot_general(sg_ref[i, head], keys, TN_DIMS, preferred_element_type=jnp.float32)
            att_ref[rows, lo:lo + HEAD] = att.astype(jnp.bfloat16)
            dq_ref[rows, lo:lo + HEAD] = dq.astype(jnp.bfloat16)


def blocks(held):
    tokens = pl.BlockSpec((BATCH * GROUP, COLS), lambda g, *_: (g, 0))
    square = pl.BlockSpec((BATCH, HEADS, SLOTS * LAT, GROUP), lambda g, *_: (g, 0, 0, 0))
    whole = pl.BlockSpec((NX, held, QUARTER, WIDE), lambda g, *_: (0, 0, 0, 0))
    return tokens, square, whole


def params(mebibytes):
    return pltpu.CompilerParams(
        dimension_semantics=("arbitrary",), vmem_limit_bytes=mebibytes * 2**20
    )


def attention(src, docs, tok, queries, grad_out, kv):
    held = kv.shape[1]
    tokens, square, whole = blocks(held)
    weights = jax.ShapeDtypeStruct((GROUPS, HEADS, SLOTS * LAT, GROUP), jnp.bfloat16)
    return pl.pallas_call(
        attention_kernel,
        grid_spec=pltpu.PrefetchScalarGridSpec(
            num_scalar_prefetch=2,
            grid=(GROUPS // BATCH,),
            in_specs=[pl.BlockSpec((BATCH, 1, GROUP), lambda g, *_: (g, 0, 0)), tokens, tokens, whole],
            out_specs=[square, square, whole],
            scratch_shapes=[pltpu.VMEM((held, LAT, WIDE), jnp.float32)],
        ),
        out_shape=[weights, weights, jax.ShapeDtypeStruct(kv.shape, jnp.bfloat16)],
        compiler_params=params(30),
        cost_estimate=pl.CostEstimate(
            flops=8 * TOKENS * GROUP * COLS, bytes_accessed=9 * 2**20, transcendentals=0
        ),
    )(src, docs, tok, queries, grad_out, kv)


def outputs(src, low, score_grad, kv):
    tokens, square, whole = blocks(kv.shape[1])
    out = jax.ShapeDtypeStruct((TOKENS, COLS), jnp.bfloat16)
    return pl.pallas_call(
        output_kernel,
        grid_spec=pltpu.PrefetchScalarGridSpec(
            num_scalar_prefetch=1,
            grid=(GROUPS // BATCH,),
            in_specs=[square, square, whole],
            out_specs=[tokens, tokens],
        ),
        out_shape=[out, out],
        compiler_params=params(20),
        cost_estimate=pl.CostEstimate(
            flops=4 * TOKENS * GROUP * COLS, bytes_accessed=8 * 2**20, transcendentals=0
        ),
    )(src, low, score_grad, kv)


def pick_kernel(index_ref, all_ref, out_ref):
    for n in range(NX * WINDOW):
        out_ref[n] = all_ref[index_ref[n]]


def add_kernel(index_ref, parts_ref, out_ref, acc):
    acc[...] = jnp.zeros_like(acc)
    for n in range(NX * WINDOW):
        acc[index_ref[n]] += parts_ref[n].astype(jnp.float32)
    out_ref[...] = acc[...].astype(jnp.bfloat16)


def by_index(kernel, index, operand, count, scratch):
    return pl.pallas_call(
        kernel,
        in_specs=[
            pl.BlockSpec(memory_space=pltpu.SMEM),
            pl.BlockSpec(memory_space=pltpu.VMEM),
        ],
        out_specs=pl.BlockSpec(memory_space=pltpu.VMEM),
        out_shape=jax.ShapeDtypeStruct((count, QUARTER, WIDE), jnp.bfloat16),
        scratch_shapes=scratch,
        compiler_params=pltpu.CompilerParams(vmem_limit_bytes=8 * 2**20),
        cost_estimate=pl.CostEstimate(flops=0, bytes_accessed=2**21, transcendentals=0),
    )(index, operand)


def gather(value, axis, size):
    copies = jnp.broadcast_to(value[None], (size,) + value.shape)
    return lax.all_to_all(copies, axis, 0, 0, tiled=True)


def lookup(slot_table, image_ids):
    matches = image_ids[..., None] == jnp.arange(IMAGES, dtype=jnp.int32)
    return jnp.sum(jnp.where(matches, slot_table, 0), axis=-1).astype(jnp.int32)


def local(queries, latents, key_weight, value_weight, grad_out, pairs, image_slot, token_doc):
    weight = jnp.concatenate([key_weight, value_weight], axis=1)
    column = gather(weight, "z", NZ).reshape(NZ * WROWS, WIDE)

    tok = token_doc.reshape(TOKENS // WIDE, WIDE)
    note = jnp.stack([jnp.min(tok, axis=0), jnp.max(tok, axis=0)]).astype(jnp.bfloat16)
    row = gather(jnp.concatenate([column, jnp.pad(note, ((0, 6), (0, 0)))]), "x", NX)
    weight = row[:, :NZ * WROWS].reshape(VIS, WIDE)
    notes = row[:, NZ * WROWS:NZ * WROWS + 2]
    starts = jnp.minimum(jnp.min(notes[:, 0], axis=-1).astype(jnp.int32), DOCS - SPAN)
    fits = jnp.max(jnp.max(notes[:, 1], axis=-1).astype(jnp.int32) - starts) < SPAN

    own = latents[0].reshape(LAT, NZ, NX, WROWS).transpose(0, 2, 1, 3).reshape(LAT, VIS)
    kv = jnp.dot(own, weight, preferred_element_type=jnp.float32).astype(jnp.bfloat16)
    kv = jnp.broadcast_to(kv.reshape(1, NX, QUARTER, WIDE), (NZ, NX, QUARTER, WIDE))
    kv = lax.all_to_all(kv.reshape(IMAGES, QUARTER, WIDE), ("z", "x"), 0, 0, tiled=True)

    docs = jnp.where(pairs >= 0, pairs // IPD, -1)
    tok = token_doc.reshape(GROUPS, 1, GROUP)
    start = lax.dynamic_index_in_dim(starts, lax.axis_index("x"), keepdims=False)
    wanted = starts[:, None] * IPD + jnp.arange(WINDOW, dtype=jnp.int32)
    wanted = lookup(image_slot, wanted).reshape(NX * WINDOW)

    def narrow():
        picked = by_index(pick_kernel, wanted, kv, NX * WINDOW, [])
        held = lax.all_to_all(picked.reshape(NX, WINDOW, QUARTER, WIDE), "x", 0, 0, tiled=True)
        src = jnp.clip(pairs - start * IPD, 0, WINDOW - 1)
        low, score_grad, dkv = attention(src, docs, tok, queries, grad_out, held)
        dkv = lax.all_to_all(dkv, "x", 0, 0, tiled=True).reshape(NX * WINDOW, QUARTER, WIDE)
        att, dq = outputs(src, low, score_grad, held)
        total = pltpu.VMEM((IMAGES, QUARTER, WIDE), jnp.float32)
        return att, dq, by_index(add_kernel, wanted, dkv, IMAGES, [total])

    def full():
        held = gather(kv, "x", NX)
        src = lookup(image_slot, pairs)
        low, score_grad, dkv = attention(src, docs, tok, queries, grad_out, held)
        att, dq = outputs(src, low, score_grad, held)
        dkv = lax.all_to_all(dkv, "x", 0, 0, tiled=True)
        return att, dq, jnp.sum(dkv.astype(jnp.float32), axis=0).astype(jnp.bfloat16)

    attended, grad_queries, dkv = lax.cond(fits, narrow, full)

    dkv = lax.all_to_all(dkv, ("z", "x"), 0, 0, tiled=True).reshape(NZ, LAT, WIDE)
    dkv = jnp.sum(dkv.astype(jnp.float32), axis=0).astype(jnp.bfloat16)

    ordered = weight.reshape(NX, NZ, WROWS, WIDE).transpose(1, 0, 2, 3).reshape(VIS, WIDE)
    term = lax.dot_general(dkv, ordered, NT_DIMS, preferred_element_type=jnp.float32)
    term = term.astype(jnp.bfloat16).reshape(NT, LAT // NT, VIS)
    term = lax.all_to_all(term, ("y", "core"), 0, 0, tiled=True)
    term = jnp.sum(term.astype(jnp.float32), axis=0).astype(jnp.bfloat16)
    term = gather(term, ("y", "core"), NT).reshape(1, LAT, VIS)
    return attended, grad_queries, term


def solution(mesh):
    fine = Mesh(mesh.devices.reshape(NZ, NX, NT // 2, 2), ("z", "x", "y", "core"))
    seq, tensor = ("z", "x"), ("y", "core")
    in_specs = (
        P(seq, tensor),
        P(seq, None, None),
        P(seq, tensor),
        P(seq, tensor),
        P(seq, tensor),
        P(seq, None),
        P(),
        P(seq),
    )
    out_specs = (P(seq, tensor), P(seq, tensor), P(seq, None, None))
    return jax.shard_map(local, mesh=fine, in_specs=in_specs, out_specs=out_specs, check_vma=False)
```

```python
import jax
import jax.numpy as jnp
from jax import lax
from jax.experimental import pallas as pl
from jax.experimental.pallas import tpu as pltpu
from jax.sharding import Mesh
from jax.sharding import PartitionSpec as P

HEAD = 128
LAT = 64
GROUP = 256
GROUPS = 8
BATCH = 4
HEADS = 2
SLOTS = 4
IPD = 4
NX = 4
NZ = 8
NT = 16
COLS = 256
WIDE = 2 * COLS
VIS = 1280
WROWS = 40
IMAGES = 32
TOKENS = 2048
DOCS = 8
QUARTER = LAT // NX
SPAN = 3
WINDOW = SPAN * IPD
MASKED = -1.0e30
SCALE = HEAD ** -0.5
LOG2E = 1.4426950408889634

NT_DIMS = (((1,), (1,)), ((), ()))
TN_DIMS = (((0,), (0,)), ((), ()))


def rows_of(kv_ref, places, lo):
    return jnp.concatenate(
        [kv_ref[part, r, :, lo:lo + HEAD] for r in places for part in range(NX)], axis=0
    )


def attention_kernel(src_ref, doc_ref, tok_ref, q_ref, g_ref, kv_ref,
                     low_ref, sg_ref, dkv_ref, acc):
    step = pl.program_id(0)

    @pl.when(step == 0)
    def _():
        acc[...] = jnp.zeros_like(acc)

    src = [[src_ref[step * BATCH + i, j] for j in range(SLOTS)] for i in range(BATCH)]
    bias = [
        [jnp.where(tok_ref[i] == doc_ref[step * BATCH + i, j], 0.0, MASKED) for j in range(SLOTS)]
        for i in range(BATCH)
    ]
    units = [(i, head * HEAD) for i in range(BATCH) for head in range(COLS // HEAD)]
    tokens = [slice(i * GROUP, (i + 1) * GROUP) for i in range(BATCH)]
    of_slot = [slice(j * LAT, (j + 1) * LAT) for j in range(SLOTS)]

    keys = [rows_of(kv_ref, src[i], lo) for i, lo in units]
    values = [rows_of(kv_ref, src[i], COLS + lo) for i, lo in units]
    queries = [q_ref[tokens[i], lo:lo + HEAD] for i, lo in units]
    grads = [g_ref[tokens[i], lo:lo + HEAD] for i, lo in units]
    scores = [
        lax.dot_general(k, q, NT_DIMS, preferred_element_type=jnp.float32)
        for k, q in zip(keys, queries)
    ]
    prob_grads = [
        lax.dot_general(v, g, NT_DIMS, preferred_element_type=jnp.float32)
        for v, g in zip(values, grads)
    ]
    lows, score_grads = [], []
    for (i, _), s, dp in zip(units, scores, prob_grads):
        s = jnp.concatenate([s[of_slot[j]] + bias[i][j] for j in range(SLOTS)], axis=0)
        top = jnp.max(s, axis=0, keepdims=True)
        e = jnp.exp2((s - top) * (SCALE * LOG2E))
        inverse = 1.0 / jnp.sum(e, axis=0, keepdims=True)
        centre = jnp.sum(e * dp, axis=0, keepdims=True) * inverse
        p = e * inverse
        lows.append(p.astype(jnp.bfloat16))
        score_grads.append((p * (dp - centre) * SCALE).astype(jnp.bfloat16))
    for u, (i, lo) in enumerate(units):
        low_ref[i, lo // HEAD] = lows[u]
        sg_ref[i, lo // HEAD] = score_grads[u]
        dk = jnp.dot(score_grads[u], queries[u], preferred_element_type=jnp.float32)
        dv = jnp.dot(lows[u], grads[u], preferred_element_type=jnp.float32)
        for j in range(SLOTS):
            acc[src[i][j], :, lo:lo + HEAD] += dk[of_slot[j]]
            acc[src[i][j], :, COLS + lo:COLS + lo + HEAD] += dv[of_slot[j]]

    @pl.when(step == GROUPS // BATCH - 1)
    def _():
        for part in range(NX):
            rows = slice(part * QUARTER, (part + 1) * QUARTER)
            dkv_ref[part] = acc[:, rows, :].astype(jnp.bfloat16)


def output_kernel(src_ref, low_ref, sg_ref, kv_ref, att_ref, dq_ref):
    step = pl.program_id(0)
    for i in range(BATCH):
        src = [src_ref[step * BATCH + i, j] for j in range(SLOTS)]
        rows = slice(i * GROUP, (i + 1) * GROUP)
        for head in range(HEADS):
            lo = head * HEAD
            keys = rows_of(kv_ref, src, lo)
            values = rows_of(kv_ref, src, COLS + lo)
            att = lax.dot_general(low_ref[i, head], values, TN_DIMS, preferred_element_type=jnp.float32)
            dq = lax.dot_general(sg_ref[i, head], keys, TN_DIMS, preferred_element_type=jnp.float32)
            att_ref[rows, lo:lo + HEAD] = att.astype(jnp.bfloat16)
            dq_ref[rows, lo:lo + HEAD] = dq.astype(jnp.bfloat16)


def blocks(held):
    tokens = pl.BlockSpec((BATCH * GROUP, COLS), lambda g, *_: (g, 0))
    square = pl.BlockSpec((BATCH, HEADS, SLOTS * LAT, GROUP), lambda g, *_: (g, 0, 0, 0))
    whole = pl.BlockSpec((NX, held, QUARTER, WIDE), lambda g, *_: (0, 0, 0, 0))
    return tokens, square, whole


def params(mebibytes):
    return pltpu.CompilerParams(
        dimension_semantics=("arbitrary",), vmem_limit_bytes=mebibytes * 2**20
    )


def attention(src, docs, tok, queries, grad_out, kv):
    held = kv.shape[1]
    tokens, square, whole = blocks(held)
    weights = pltpu.HBM((GROUPS, HEADS, SLOTS * LAT, GROUP), jnp.bfloat16)
    return pl.pallas_call(
        attention_kernel,
        grid_spec=pltpu.PrefetchScalarGridSpec(
            num_scalar_prefetch=2,
            grid=(GROUPS // BATCH,),
            in_specs=[pl.BlockSpec((BATCH, 1, GROUP), lambda g, *_: (g, 0, 0)), tokens, tokens, whole],
            out_specs=[square, square, whole],
            scratch_shapes=[pltpu.VMEM((held, LAT, WIDE), jnp.float32)],
        ),
        out_shape=[weights, weights, jax.ShapeDtypeStruct(kv.shape, jnp.bfloat16)],
        compiler_params=params(30),
        cost_estimate=pl.CostEstimate(
            flops=8 * TOKENS * GROUP * COLS, bytes_accessed=9 * 2**20, transcendentals=0
        ),
    )(src, docs, tok, queries, grad_out, kv)


def outputs(src, low, score_grad, kv):
    tokens, square, whole = blocks(kv.shape[1])
    out = jax.ShapeDtypeStruct((TOKENS, COLS), jnp.bfloat16)
    return pl.pallas_call(
        output_kernel,
        grid_spec=pltpu.PrefetchScalarGridSpec(
            num_scalar_prefetch=1,
            grid=(GROUPS // BATCH,),
            in_specs=[square, square, whole],
            out_specs=[tokens, tokens],
        ),
        out_shape=[out, out],
        compiler_params=params(20),
        cost_estimate=pl.CostEstimate(
            flops=4 * TOKENS * GROUP * COLS, bytes_accessed=8 * 2**20, transcendentals=0
        ),
    )(src, low, score_grad, kv)


def pick_kernel(index_ref, all_ref, out_ref):
    for n in range(NX * WINDOW):
        out_ref[n] = all_ref[index_ref[n]]


def add_kernel(index_ref, parts_ref, out_ref, acc):
    acc[...] = jnp.zeros_like(acc)
    for n in range(NX * WINDOW):
        acc[index_ref[n]] += parts_ref[n].astype(jnp.float32)
    out_ref[...] = acc[...].astype(jnp.bfloat16)


def by_index(kernel, index, operand, count, scratch):
    return pl.pallas_call(
        kernel,
        in_specs=[
            pl.BlockSpec(memory_space=pltpu.SMEM),
            pl.BlockSpec(memory_space=pltpu.VMEM),
        ],
        out_specs=pl.BlockSpec(memory_space=pltpu.VMEM),
        out_shape=jax.ShapeDtypeStruct((count, QUARTER, WIDE), jnp.bfloat16),
        scratch_shapes=scratch,
        compiler_params=pltpu.CompilerParams(vmem_limit_bytes=8 * 2**20),
        cost_estimate=pl.CostEstimate(flops=0, bytes_accessed=2**21, transcendentals=0),
    )(index, operand)


def gather(value, axis, size):
    copies = jnp.broadcast_to(value[None], (size,) + value.shape)
    return lax.all_to_all(copies, axis, 0, 0, tiled=True)


def lookup(slot_table, image_ids):
    matches = image_ids[..., None] == jnp.arange(IMAGES, dtype=jnp.int32)
    return jnp.sum(jnp.where(matches, slot_table, 0), axis=-1).astype(jnp.int32)


def local(queries, latents, key_weight, value_weight, grad_out, pairs, image_slot, token_doc):
    weight = jnp.concatenate([key_weight, value_weight], axis=1)
    column = gather(weight, "z", NZ).reshape(NZ * WROWS, WIDE)

    tok = token_doc.reshape(TOKENS // WIDE, WIDE)
    note = jnp.stack([jnp.min(tok, axis=0), jnp.max(tok, axis=0)]).astype(jnp.bfloat16)
    row = gather(jnp.concatenate([column, jnp.pad(note, ((0, 6), (0, 0)))]), "x", NX)
    weight = row[:, :NZ * WROWS].reshape(VIS, WIDE)
    notes = row[:, NZ * WROWS:NZ * WROWS + 2]
    starts = jnp.minimum(jnp.min(notes[:, 0], axis=-1).astype(jnp.int32), DOCS - SPAN)
    fits = jnp.max(jnp.max(notes[:, 1], axis=-1).astype(jnp.int32) - starts) < SPAN

    own = latents[0].reshape(LAT, NZ, NX, WROWS).transpose(0, 2, 1, 3).reshape(LAT, VIS)
    kv = jnp.dot(own, weight, preferred_element_type=jnp.float32).astype(jnp.bfloat16)
    kv = jnp.broadcast_to(kv.reshape(1, NX, QUARTER, WIDE), (NZ, NX, QUARTER, WIDE))
    kv = lax.all_to_all(kv.reshape(IMAGES, QUARTER, WIDE), ("z", "x"), 0, 0, tiled=True)

    docs = jnp.where(pairs >= 0, pairs // IPD, -1)
    tok = token_doc.reshape(GROUPS, 1, GROUP)
    start = lax.dynamic_index_in_dim(starts, lax.axis_index("x"), keepdims=False)
    wanted = starts[:, None] * IPD + jnp.arange(WINDOW, dtype=jnp.int32)
    wanted = lookup(image_slot, wanted).reshape(NX * WINDOW)

    def narrow():
        picked = by_index(pick_kernel, wanted, kv, NX * WINDOW, [])
        held = lax.all_to_all(picked.reshape(NX, WINDOW, QUARTER, WIDE), "x", 0, 0, tiled=True)
        src = jnp.clip(pairs - start * IPD, 0, WINDOW - 1)
        low, score_grad, dkv = attention(src, docs, tok, queries, grad_out, held)
        dkv = lax.all_to_all(dkv, "x", 0, 0, tiled=True).reshape(NX * WINDOW, QUARTER, WIDE)
        att, dq = outputs(src, low, score_grad, held)
        total = pltpu.VMEM((IMAGES, QUARTER, WIDE), jnp.float32)
        return att, dq, by_index(add_kernel, wanted, dkv, IMAGES, [total])

    def full():
        held = gather(kv, "x", NX)
        src = lookup(image_slot, pairs)
        low, score_grad, dkv = attention(src, docs, tok, queries, grad_out, held)
        att, dq = outputs(src, low, score_grad, held)
        dkv = lax.all_to_all(dkv, "x", 0, 0, tiled=True)
        return att, dq, jnp.sum(dkv.astype(jnp.float32), axis=0).astype(jnp.bfloat16)

    attended, grad_queries, dkv = lax.cond(fits, narrow, full)

    dkv = lax.all_to_all(dkv, ("z", "x"), 0, 0, tiled=True).reshape(NZ, LAT, WIDE)
    dkv = jnp.sum(dkv.astype(jnp.float32), axis=0).astype(jnp.bfloat16)

    ordered = weight.reshape(NX, NZ, WROWS, WIDE).transpose(1, 0, 2, 3).reshape(VIS, WIDE)
    term = lax.dot_general(dkv, ordered, NT_DIMS, preferred_element_type=jnp.float32)
    term = term.astype(jnp.bfloat16).reshape(NT, LAT // NT, VIS)
    term = lax.all_to_all(term, ("y", "core"), 0, 0, tiled=True)
    term = jnp.sum(term.astype(jnp.float32), axis=0).astype(jnp.bfloat16)
    term = gather(term, ("y", "core"), NT).reshape(1, LAT, VIS)
    return attended, grad_queries, term


def solution(mesh):
    fine = Mesh(mesh.devices.reshape(NZ, NX, NT // 2, 2), ("z", "x", "y", "core"))
    seq, tensor = ("z", "x"), ("y", "core")
    in_specs = (
        P(seq, tensor),
        P(seq, None, None),
        P(seq, tensor),
        P(seq, tensor),
        P(seq, tensor),
        P(seq, None),
        P(),
        P(seq),
    )
    out_specs = (P(seq, tensor), P(seq, tensor), P(seq, None, None))
    return jax.shard_map(local, mesh=fine, in_specs=in_specs, out_specs=out_specs, check_vma=False)
```

```python
import jax
import jax.numpy as jnp
from jax import lax
from jax.experimental import pallas as pl
from jax.experimental.pallas import tpu as pltpu
from jax.sharding import Mesh
from jax.sharding import PartitionSpec as P

HEAD = 128
LAT = 64
GROUP = 256
GROUPS = 8
BATCH = 2
HEADS = 2
SLOTS = 4
IPD = 4
NX = 4
NZ = 8
NT = 16
COLS = 256
WIDE = 2 * COLS
VIS = 1280
WROWS = 40
IMAGES = 32
TOKENS = 2048
DOCS = 8
QUARTER = LAT // NX
SPAN = 3
WINDOW = SPAN * IPD
MASKED = -1.0e30
SCALE = HEAD ** -0.5
LOG2E = 1.4426950408889634

NT_DIMS = (((1,), (1,)), ((), ()))
TN_DIMS = (((0,), (0,)), ((), ()))


def rows_of(kv_ref, places, lo):
    return jnp.concatenate(
        [kv_ref[part, r, :, lo:lo + HEAD] for r in places for part in range(NX)], axis=0
    )


def attention_kernel(src_ref, doc_ref, tok_ref, q_ref, g_ref, kv_ref,
                     low_ref, sg_ref, dkv_ref, acc):
    step = pl.program_id(0)

    @pl.when(step == 0)
    def _():
        acc[...] = jnp.zeros_like(acc)

    src = [[src_ref[step * BATCH + i, j] for j in range(SLOTS)] for i in range(BATCH)]
    bias = [
        [jnp.where(tok_ref[i] == doc_ref[step * BATCH + i, j], 0.0, MASKED) for j in range(SLOTS)]
        for i in range(BATCH)
    ]
    units = [(i, head * HEAD) for i in range(BATCH) for head in range(COLS // HEAD)]
    tokens = [slice(i * GROUP, (i + 1) * GROUP) for i in range(BATCH)]
    of_slot = [slice(j * LAT, (j + 1) * LAT) for j in range(SLOTS)]

    keys = [rows_of(kv_ref, src[i], lo) for i, lo in units]
    values = [rows_of(kv_ref, src[i], COLS + lo) for i, lo in units]
    queries = [q_ref[tokens[i], lo:lo + HEAD] for i, lo in units]
    grads = [g_ref[tokens[i], lo:lo + HEAD] for i, lo in units]
    scores = [
        lax.dot_general(k, q, NT_DIMS, preferred_element_type=jnp.float32)
        for k, q in zip(keys, queries)
    ]
    prob_grads = [
        lax.dot_general(v, g, NT_DIMS, preferred_element_type=jnp.float32)
        for v, g in zip(values, grads)
    ]
    lows, score_grads = [], []
    for (i, _), s, dp in zip(units, scores, prob_grads):
        s = jnp.concatenate([s[of_slot[j]] + bias[i][j] for j in range(SLOTS)], axis=0)
        top = jnp.max(s, axis=0, keepdims=True)
        e = jnp.exp2((s - top) * (SCALE * LOG2E))
        inverse = 1.0 / jnp.sum(e, axis=0, keepdims=True)
        centre = jnp.sum(e * dp, axis=0, keepdims=True) * inverse
        p = e * inverse
        lows.append(p.astype(jnp.bfloat16))
        score_grads.append((p * (dp - centre) * SCALE).astype(jnp.bfloat16))
    for u, (i, lo) in enumerate(units):
        low_ref[i, lo // HEAD] = lows[u]
        sg_ref[i, lo // HEAD] = score_grads[u]
        dk = jnp.dot(score_grads[u], queries[u], preferred_element_type=jnp.float32)
        dv = jnp.dot(lows[u], grads[u], preferred_element_type=jnp.float32)
        for j in range(SLOTS):
            acc[src[i][j], :, lo:lo + HEAD] += dk[of_slot[j]]
            acc[src[i][j], :, COLS + lo:COLS + lo + HEAD] += dv[of_slot[j]]

    @pl.when(step == GROUPS // BATCH - 1)
    def _():
        for part in range(NX):
            rows = slice(part * QUARTER, (part + 1) * QUARTER)
            dkv_ref[part] = acc[:, rows, :].astype(jnp.bfloat16)


def output_kernel(src_ref, low_ref, sg_ref, kv_ref, att_ref, dq_ref):
    step = pl.program_id(0)
    for i in range(BATCH):
        src = [src_ref[step * BATCH + i, j] for j in range(SLOTS)]
        rows = slice(i * GROUP, (i + 1) * GROUP)
        for head in range(HEADS):
            lo = head * HEAD
            keys = rows_of(kv_ref, src, lo)
            values = rows_of(kv_ref, src, COLS + lo)
            att = lax.dot_general(low_ref[i, head], values, TN_DIMS, preferred_element_type=jnp.float32)
            dq = lax.dot_general(sg_ref[i, head], keys, TN_DIMS, preferred_element_type=jnp.float32)
            att_ref[rows, lo:lo + HEAD] = att.astype(jnp.bfloat16)
            dq_ref[rows, lo:lo + HEAD] = dq.astype(jnp.bfloat16)


def blocks(held):
    tokens = pl.BlockSpec((BATCH * GROUP, COLS), lambda g, *_: (g, 0))
    square = pl.BlockSpec((BATCH, HEADS, SLOTS * LAT, GROUP), lambda g, *_: (g, 0, 0, 0))
    whole = pl.BlockSpec(
        (NX, held, QUARTER, WIDE), lambda g, *_: (0, 0, 0, 0), pipeline_mode=pl.Buffered(1)
    )
    return tokens, square, whole


def params(mebibytes):
    return pltpu.CompilerParams(
        dimension_semantics=("arbitrary",), vmem_limit_bytes=mebibytes * 2**20
    )


def attention(src, docs, tok, queries, grad_out, kv):
    held = kv.shape[1]
    tokens, square, whole = blocks(held)
    weights = pltpu.HBM((GROUPS, HEADS, SLOTS * LAT, GROUP), jnp.bfloat16)
    return pl.pallas_call(
        attention_kernel,
        grid_spec=pltpu.PrefetchScalarGridSpec(
            num_scalar_prefetch=2,
            grid=(GROUPS // BATCH,),
            in_specs=[pl.BlockSpec((BATCH, 1, GROUP), lambda g, *_: (g, 0, 0)), tokens, tokens, whole],
            out_specs=[square, square, whole],
            scratch_shapes=[pltpu.VMEM((held, LAT, WIDE), jnp.float32)],
        ),
        out_shape=[weights, weights, jax.ShapeDtypeStruct(kv.shape, jnp.bfloat16)],
        compiler_params=params(30),
        cost_estimate=pl.CostEstimate(
            flops=8 * TOKENS * GROUP * COLS, bytes_accessed=9 * 2**20, transcendentals=0
        ),
    )(src, docs, tok, queries, grad_out, kv)


def outputs(src, low, score_grad, kv):
    tokens, square, whole = blocks(kv.shape[1])
    out = jax.ShapeDtypeStruct((TOKENS, COLS), jnp.bfloat16)
    return pl.pallas_call(
        output_kernel,
        grid_spec=pltpu.PrefetchScalarGridSpec(
            num_scalar_prefetch=1,
            grid=(GROUPS // BATCH,),
            in_specs=[square, square, whole],
            out_specs=[tokens, tokens],
        ),
        out_shape=[out, out],
        compiler_params=params(20),
        cost_estimate=pl.CostEstimate(
            flops=4 * TOKENS * GROUP * COLS, bytes_accessed=8 * 2**20, transcendentals=0
        ),
    )(src, low, score_grad, kv)


def pick_kernel(index_ref, all_ref, out_ref):
    for n in range(NX * WINDOW):
        out_ref[n] = all_ref[index_ref[n]]


def add_kernel(index_ref, parts_ref, out_ref, acc):
    acc[...] = jnp.zeros_like(acc)
    for n in range(NX * WINDOW):
        acc[index_ref[n]] += parts_ref[n].astype(jnp.float32)
    out_ref[...] = acc[...].astype(jnp.bfloat16)


def by_index(kernel, index, operand, count, scratch):
    return pl.pallas_call(
        kernel,
        in_specs=[
            pl.BlockSpec(memory_space=pltpu.SMEM),
            pl.BlockSpec(memory_space=pltpu.VMEM),
        ],
        out_specs=pl.BlockSpec(memory_space=pltpu.VMEM),
        out_shape=jax.ShapeDtypeStruct((count, QUARTER, WIDE), jnp.bfloat16),
        scratch_shapes=scratch,
        compiler_params=pltpu.CompilerParams(vmem_limit_bytes=8 * 2**20),
        cost_estimate=pl.CostEstimate(flops=0, bytes_accessed=2**21, transcendentals=0),
    )(index, operand)


def gather(value, axis, size):
    copies = jnp.broadcast_to(value[None], (size,) + value.shape)
    return lax.all_to_all(copies, axis, 0, 0, tiled=True)


def lookup(slot_table, image_ids):
    matches = image_ids[..., None] == jnp.arange(IMAGES, dtype=jnp.int32)
    return jnp.sum(jnp.where(matches, slot_table, 0), axis=-1).astype(jnp.int32)


def local(queries, latents, key_weight, value_weight, grad_out, pairs, image_slot, token_doc):
    weight = jnp.concatenate([key_weight, value_weight], axis=1)
    column = gather(weight, "z", NZ).reshape(NZ * WROWS, WIDE)

    tok = token_doc.reshape(TOKENS // WIDE, WIDE)
    note = jnp.stack([jnp.min(tok, axis=0), jnp.max(tok, axis=0)]).astype(jnp.bfloat16)
    row = gather(jnp.concatenate([column, jnp.pad(note, ((0, 6), (0, 0)))]), "x", NX)
    weight = row[:, :NZ * WROWS].reshape(VIS, WIDE)
    notes = row[:, NZ * WROWS:NZ * WROWS + 2]
    starts = jnp.minimum(jnp.min(notes[:, 0], axis=-1).astype(jnp.int32), DOCS - SPAN)
    fits = jnp.max(jnp.max(notes[:, 1], axis=-1).astype(jnp.int32) - starts) < SPAN

    own = latents[0].reshape(LAT, NZ, NX, WROWS).transpose(0, 2, 1, 3).reshape(LAT, VIS)
    kv = jnp.dot(own, weight, preferred_element_type=jnp.float32).astype(jnp.bfloat16)
    kv = jnp.broadcast_to(kv.reshape(1, NX, QUARTER, WIDE), (NZ, NX, QUARTER, WIDE))
    kv = lax.all_to_all(kv.reshape(IMAGES, QUARTER, WIDE), ("z", "x"), 0, 0, tiled=True)

    docs = jnp.where(pairs >= 0, pairs // IPD, -1)
    tok = token_doc.reshape(GROUPS, 1, GROUP)
    start = lax.dynamic_index_in_dim(starts, lax.axis_index("x"), keepdims=False)
    wanted = starts[:, None] * IPD + jnp.arange(WINDOW, dtype=jnp.int32)
    wanted = lookup(image_slot, wanted).reshape(NX * WINDOW)

    def narrow():
        picked = by_index(pick_kernel, wanted, kv, NX * WINDOW, [])
        held = lax.all_to_all(picked.reshape(NX, WINDOW, QUARTER, WIDE), "x", 0, 0, tiled=True)
        src = jnp.clip(pairs - start * IPD, 0, WINDOW - 1)
        low, score_grad, dkv = attention(src, docs, tok, queries, grad_out, held)
        dkv = lax.all_to_all(dkv, "x", 0, 0, tiled=True).reshape(NX * WINDOW, QUARTER, WIDE)
        att, dq = outputs(src, low, score_grad, held)
        total = pltpu.VMEM((IMAGES, QUARTER, WIDE), jnp.float32)
        return att, dq, by_index(add_kernel, wanted, dkv, IMAGES, [total])

    def full():
        held = gather(kv, "x", NX)
        src = lookup(image_slot, pairs)
        low, score_grad, dkv = attention(src, docs, tok, queries, grad_out, held)
        att, dq = outputs(src, low, score_grad, held)
        dkv = lax.all_to_all(dkv, "x", 0, 0, tiled=True)
        return att, dq, jnp.sum(dkv.astype(jnp.float32), axis=0).astype(jnp.bfloat16)

    attended, grad_queries, dkv = lax.cond(fits, narrow, full)

    dkv = lax.all_to_all(dkv, ("z", "x"), 0, 0, tiled=True).reshape(NZ, LAT, WIDE)
    dkv = jnp.sum(dkv.astype(jnp.float32), axis=0).astype(jnp.bfloat16)

    ordered = weight.reshape(NX, NZ, WROWS, WIDE).transpose(1, 0, 2, 3).reshape(VIS, WIDE)
    term = lax.dot_general(dkv, ordered, NT_DIMS, preferred_element_type=jnp.float32)
    term = term.astype(jnp.bfloat16).reshape(NT, LAT // NT, VIS)
    term = lax.all_to_all(term, ("y", "core"), 0, 0, tiled=True)
    term = jnp.sum(term.astype(jnp.float32), axis=0).astype(jnp.bfloat16)
    term = gather(term, ("y", "core"), NT).reshape(1, LAT, VIS)
    return attended, grad_queries, term


def solution(mesh):
    fine = Mesh(mesh.devices.reshape(NZ, NX, NT // 2, 2), ("z", "x", "y", "core"))
    seq, tensor = ("z", "x"), ("y", "core")
    in_specs = (
        P(seq, tensor),
        P(seq, None, None),
        P(seq, tensor),
        P(seq, tensor),
        P(seq, tensor),
        P(seq, None),
        P(),
        P(seq),
    )
    out_specs = (P(seq, tensor), P(seq, tensor), P(seq, None, None))
    return jax.shard_map(local, mesh=fine, in_specs=in_specs, out_specs=out_specs, check_vma=False)
```
